256 devices in a mesh: pb: 8 (over z_lo, y), ka: 32 (over z_hi, x, core).
Axes of the slice: x: 4, y: 4, z: 8 (z_hi: 4, z_lo: 2; z = z_hi * 2 + z_lo), core: 2. Of those that a mesh axis runs over, the one named last changes fastest.
Arguments:
- query_features: bfloat16 [32768, 128], P(('pb', 'ka')), may hold values from -240 to 240, as said below
- key_features: bfloat16 [131072, 128], P(('ka', 'pb')), may hold values from -16 to 16, as said below
Outputs:
- forward_flow: float32 [2, 32768], P(None, ('pb', 'ka'))
- backward_flow: float32 [2, 131072], P(None, ('ka', 'pb'))
The draws below stay inside these ranges and needn't reach their ends.
Inputs may be any that keep to these rules, and one draw needn't show every extreme that they name: `query_features`: finite feature values. `key_features`: finite feature values.
All inputs are finite; a program needn't handle non-finite values.
Results may differ from the reference program's by a relative error of at most 0.0009.
Values may be sent and summed in bfloat16 or wider, within the bound.
No kernel may reach another device: no remote copies, remote signals or barrier semaphores. Data moves between devices by JAX's collectives and lax.ppermute only.
A program may use at most 192 MiB of HBM per device.

```python
import jax
import jax.numpy as jnp
from jax import lax

C = 128
FRAME_W = 480
NQ = 32768
NK = 131072


def shared_base(key):
    base = jnp.clip(jax.random.normal(jax.random.fold_in(key, 11), (NK, C), jnp.float32), -6.0, 6.0)
    return base


def draw_key_features(key, part):
    base = shared_base(key)
    return (1.3 * base).astype(jnp.bfloat16)


def draw_query_features(key, part):
    base = shared_base(key)
    key = jax.random.fold_in(key, 5)
    first = jax.random.randint(jax.random.fold_in(key, 1), (NQ,), 0, NK)
    second = jax.random.randint(jax.random.fold_in(key, 2), (NQ,), 0, NK)
    ratio = jax.random.uniform(jax.random.fold_in(key, 3), (NQ, 1), jnp.float32, 0.85, 0.95)
    noise = 0.5 * jax.random.normal(jax.random.fold_in(key, 4), (NQ, C), jnp.float32)
    strength = 1.3
    values = strength * (base[first] + ratio * base[second]) + noise
    return values.astype(jnp.bfloat16)


def setup_inputs(seed: int = 0) -> dict:
    arg_keys = jax.random.split(jax.random.key(seed), 3)
    query_features = draw_query_features(jax.random.fold_in(arg_keys[2], 71), 0)
    key_features = draw_key_features(jax.random.fold_in(arg_keys[2], 71), 0)
    return {"query_features": query_features, "key_features": key_features}


def reference(query_features, key_features):
    scale = 1.0 / (C ** 0.5)
    block = min(512, NQ)
    count = NQ // block
    key_index = jnp.arange(NK, dtype=jnp.int32)
    key_x = (key_index % FRAME_W).astype(jnp.float32) / FRAME_W
    key_y = (key_index // FRAME_W).astype(jnp.float32) / FRAME_W
    blocks = query_features.reshape(count, block, C)

    def step(carry, item):
        col_max, col_sum, col_x, col_y = carry
        number, rows = item
        query_index = number * block + jnp.arange(block, dtype=jnp.int32)
        query_x = (query_index % FRAME_W).astype(jnp.float32) / FRAME_W
        query_y = (query_index // FRAME_W).astype(jnp.float32) / FRAME_W
        score = jnp.dot(rows, key_features.T, preferred_element_type=jnp.float32) * scale
        row_max = jnp.max(score, axis=1)
        weights = jnp.exp(score - row_max[:, None])
        row_sum = jnp.sum(weights, axis=1)
        flow_x = jnp.sum(weights * key_x[None, :], axis=1) / row_sum - query_x
        flow_y = jnp.sum(weights * key_y[None, :], axis=1) / row_sum - query_y
        top = jnp.maximum(col_max, jnp.max(score, axis=0))
        factor = jnp.exp(col_max - top)
        col_weights = jnp.exp(score - top[None, :])
        col_sum = col_sum * factor + jnp.sum(col_weights, axis=0)
        col_x = col_x * factor + jnp.sum(col_weights * query_x[:, None], axis=0)
        col_y = col_y * factor + jnp.sum(col_weights * query_y[:, None], axis=0)
        return (top, col_sum, col_x, col_y), (flow_x, flow_y)

    start = (jnp.full((NK,), -jnp.inf, jnp.float32), jnp.zeros((NK,), jnp.float32),
             jnp.zeros((NK,), jnp.float32), jnp.zeros((NK,), jnp.float32))
    final, flows = lax.scan(step, start, (jnp.arange(count, dtype=jnp.int32), blocks))
    forward_flow = jnp.stack([flows[0].reshape(NQ), flows[1].reshape(NQ)])
    col_max, col_sum, col_x, col_y = final
    backward_flow = jnp.stack([col_x / col_sum - key_x, col_y / col_sum - key_y])
    return forward_flow, backward_flow
```

```python
import functools
import math

import jax
import jax.numpy as jnp
from jax import lax
from jax.experimental import pallas as pl
from jax.experimental.pallas import tpu as pltpu
from jax.sharding import Mesh
from jax.sharding import PartitionSpec as P

FRAME_W = 480
CH = 128
NPIECE, PIECE = 8, 512
GROUP = 16
RUN = 32
TILES = 4
SCALE = math.log2(math.e) / math.sqrt(CH)
LOW, HIGH = 2.0**-90, 2.0**100
AXES = ("zl", "y", "zh", "x", "core")
SIZES = {"zl": 2, "y": 4, "zh": 4, "x": 4, "core": 2}
NT = (((1,), (1,)), ((), ()))


def nt_dot(a, b):
    return lax.dot_general(a, b, NT, preferred_element_type=jnp.float32)


def split2(v):
    high = v.astype(jnp.bfloat16)
    return high, (v - high.astype(jnp.float32)).astype(jnp.bfloat16)


def cell(n):
    y = ((n >> 5) * 4370) >> 16
    return (n - y * FRAME_W).astype(jnp.float32), y.astype(jnp.float32)


def iota(shape, axis):
    return lax.broadcasted_iota(jnp.int32, shape, axis)


def query_weights(sc, half):
    lane = iota((16, 256), 1)
    row = iota((16, 256), 0)
    on_sum = lane < 128
    lane = lane & 127
    s, g = lane >> 3, lane & 7
    shard = ((sc[2] * 4 + (s >> 2)) * 4 + sc[3]) * 8 + (s & 3) * 2 + half
    x, y = cell(shard * 128 + g * GROUP)
    value = jnp.where(
        row == 0, 1.0, jnp.where(row == 1, x + (GROUP - 256.0), jnp.where(row == 2, y, 0.0))
    )
    value = jnp.where(on_sum, value, jnp.where(row == 1, -1.0, 0.0))
    return value.astype(jnp.bfloat16)


def key_weights(sc, piece, half):
    x, y = cell(sc[8 + piece] + half * 256 + iota((8, 128), 0) * RUN)
    return x + (RUN - 256.0), y - 128.0


def unpack_rows(row_ref, values, half, stat):
    lane = iota((16, 128), 1) >> 3
    out = jnp.zeros((16, 128), jnp.float32)
    for t in range(GROUP):
        spread = jnp.broadcast_to(values[t : t + 1, :], (16, 128))
        turned = pltpu.roll(pltpu.roll(spread, 0, 1, stride=8, stride_axis=0), (t * 8 + 8) % 128, 1)
        out = jnp.where(lane == t, turned, out)
    for s in range(16):
        row_ref[half * 16 + s, stat : stat + 1, :] = out[15 - s : 16 - s, :]


def main_kernel(sc, qa, qb, *refs):
    k_refs = refs[:NPIECE]
    row_ref, col_ref, qf, qp, kk, acc, sums_ref, moments_ref, rm, km = refs[NPIECE:]

    def place(j, carry):
        slot = (j ^ sc[1]) * 128
        a = pl.multiple_of(sc[0] * 2048 + slot, 128)
        b = pl.multiple_of((1 - sc[0]) * 2048 + slot, 128)
        src = pl.ds(pl.multiple_of(j * 128, 128), 128)
        qf[pl.ds(a, 128), :] = qa[src, :].astype(jnp.float32)
        qf[pl.ds(b, 128), :] = qb[src, :].astype(jnp.float32)
        return carry

    lax.fori_loop(0, 16, place, 0)

    def tile(t, carry):
        for half in range(2):
            rows = [qf[pl.ds(half * 2048 + s * 128 + t, 8, stride=16), :] for s in range(16)]
            at = pl.multiple_of(half * 2048 + t * 128, 128)
            qp[pl.ds(at, 128), :] = jnp.concatenate(rows, 0).astype(jnp.bfloat16)
        return carry

    lax.fori_loop(0, GROUP, tile, 0, unroll=2)

    r, c = iota((256, 256), 0), iota((256, 256), 1)
    perm = jnp.where(c == (r & 7) * RUN + (r >> 3), 1.0, 0.0).astype(jnp.bfloat16)
    for piece in range(NPIECE):
        for half in range(2):
            at = piece * PIECE + half * 256
            kk[at : at + 256, :] = jnp.dot(
                perm, k_refs[piece][half * 256 : half * 256 + 256, :],
                preferred_element_type=jnp.float32,
            ).astype(jnp.bfloat16)

    def score(piece, half, lanes):
        at = pl.multiple_of(piece * PIECE + half * 256, 256)
        return nt_dot(kk[pl.ds(at, 256), :], qp[lanes, :]) * SCALE

    def stats(shifted):
        tiles = 1 if shifted else TILES
        acc[...] = jnp.zeros_like(acc)

        def one_piece(piece, carry):
            total = jnp.zeros((16, PIECE), jnp.float32)
            for side in range(2):
                sums_ref[...] = jnp.zeros_like(sums_ref)
                moments_ref[...] = jnp.zeros_like(moments_ref)

                def chunk(j, carry):
                    at = pl.multiple_of(side * 2048 + j * tiles * 128, tiles * 128)
                    lanes = pl.ds(at, tiles * 128)
                    for half in range(2):
                        s = score(piece, half, lanes)
                        if shifted:
                            top = km[pl.ds(pl.multiple_of(piece * PIECE + half * 256, 256), 256), :]
                            for_key = jnp.exp2(s - top)
                            for_query = jnp.exp2(s - rm[0:1, lanes])
                        else:
                            for_key = for_query = jnp.exp2(s)
                        sums, moments = [None] * tiles, [None] * tiles
                        for u in range(RUN):
                            rows = slice(half * 256 + u * 8, half * 256 + u * 8 + 8)
                            key_sum, key_moment = sums_ref[rows, :], moments_ref[rows, :]
                            for i in range(tiles):
                                part = (slice(u * 8, u * 8 + 8), slice(i * 128, i * 128 + 128))
                                e = for_query[part]
                                sums[i] = e if u == 0 else sums[i] + e
                                moments[i] = sums[i] if u == 0 else moments[i] + sums[i]
                                key_sum = key_sum + for_key[part]
                                key_moment = key_moment + key_sum
                            sums_ref[rows, :] = key_sum
                            moments_ref[rows, :] = key_moment
                        x, y = key_weights(sc, piece, half)
                        for i in range(tiles):
                            d = pl.ds(pl.multiple_of(at + i * 128, 128), 128)
                            acc[0, :, d] += sums[i]
                            acc[1, :, d] += sums[i] * x - moments[i]
                            acc[2, :, d] += sums[i] * y
                    return carry

                lax.fori_loop(0, GROUP // tiles, chunk, 0, unroll=1 if shifted else GROUP // tiles)
                w = query_weights(sc, side)
                for j in range(16):
                    half, run = j // 8, j % 8
                    there = pl.ds(half * 256 + run, RUN, stride=8)
                    v = jnp.concatenate([sums_ref[there, :], moments_ref[there, :]], 1)
                    hi, lo = split2(v)
                    if j % 4 == 0:
                        his, los = [], []
                    his.append(hi)
                    los.append(lo)
                    if j % 4 == 3:
                        a = (j // 4) * 128
                        got = nt_dot(w, jnp.concatenate(his, 0)) + nt_dot(w, jnp.concatenate(los, 0))
                        if side == 0:
                            col_ref[sc[16 + piece], 0:3, a : a + 128] = got[0:3]
                        else:
                            col_ref[sc[16 + piece], 0:3, a : a + 128] += got[0:3]
            if not shifted:
                col_ref[sc[16 + piece], 3:4, :] = jnp.zeros((1, PIECE), jnp.float32)
            return carry

        lax.fori_loop(0, NPIECE, one_piece, 0)
        for side in range(2):
            for stat in range(4):
                parts = []
                for t in range(GROUP):
                    d = slice(side * 2048 + t * 128, side * 2048 + t * 128 + 128)
                    if stat < 3:
                        parts.append(jnp.sum(acc[stat, :, d], axis=0, keepdims=True))
                    elif shifted:
                        parts.append(rm[0:1, d])
                if parts:
                    unpack_rows(row_ref, jnp.concatenate(parts, 0), side, stat)
                else:
                    row_ref[:, 3:4, :] = jnp.zeros((32, 1, 128), jnp.float32)

    stats(False)
    row_sums, col_sums = row_ref[:, 0, :], col_ref[:, 0, :]
    low = jnp.minimum(jnp.min(row_sums), jnp.min(col_sums))
    high = jnp.maximum(jnp.max(row_sums), jnp.max(col_sums))

    @pl.when(jnp.logical_not((low > LOW) & (high < HIGH)))
    def _():
        rm[...] = jnp.full_like(rm, -jnp.inf)

        def block(j, carry):
            piece, half = j >> 1, j & 1
            at = pl.multiple_of(j * 256, 256)

            def chunk(t, top):
                lanes = pl.ds(pl.multiple_of(t * 128, 128), 128)
                s = score(piece, half, lanes)
                rm[:, lanes] = jnp.maximum(rm[:, lanes], jnp.max(s.reshape(RUN, 8, 128), axis=0))
                return jnp.maximum(top, s)

            top = lax.fori_loop(
                0, 32, chunk, jnp.full((256, 128), -jnp.inf, jnp.float32)
            )
            top = jnp.max(top, axis=1, keepdims=True)
            hi, lo = split2(jnp.broadcast_to(top, (256, 128)))
            km[pl.ds(at, 256), :] = hi.astype(jnp.float32) + lo.astype(jnp.float32)
            return carry

        lax.fori_loop(0, 2 * NPIECE, block, 0)
        rm[...] = jnp.broadcast_to(jnp.max(rm[...], axis=0, keepdims=True), rm.shape)
        pick = jnp.where((iota((16, 128), 0) == 0) & (iota((16, 128), 1) == 0), 1.0, 0.0)
        pick = pick.astype(jnp.bfloat16)

        def tops(piece, carry):
            for j in range(16):
                half, run = j // 8, j % 8
                v = km[pl.ds(piece * PIECE + half * 256 + run, RUN, stride=8), :]
                hi, lo = split2(v)
                if j % 4 == 0:
                    his, los = [], []
                his.append(hi)
                los.append(lo)
                if j % 4 == 3:
                    a = (j // 4) * 128
                    got = nt_dot(pick, jnp.concatenate(his, 0)) + nt_dot(pick, jnp.concatenate(los, 0))
                    col_ref[sc[16 + piece], 3:4, a : a + 128] = got[0:1]
            return carry

        lax.fori_loop(0, NPIECE, tops, 0)
        stats(True)


def final_kernel(sc, rows, cols, f_ref, b_ref):
    def merged(parts, count):
        top = parts[0][3:4]
        for j in range(1, count):
            top = jnp.maximum(top, parts[j][3:4])
        total = None
        for j in range(count):
            v = parts[j][0:3] * jnp.exp2(parts[j][3:4] - top)
            total = v if total is None else total + v
        return total

    q = merged([rows[j] for j in range(32)], 32)
    n = sc[0] + (iota((1, 128), 1) & 7) * GROUP + (iota((1, 128), 1) >> 3)
    x, y = cell(n)
    fx = (q[1:2] / q[0:1] + (256.0 - x)) / FRAME_W
    fy = (q[2:3] / q[0:1] + (128.0 - y)) / FRAME_W
    r, c = iota((128, 128), 0), iota((128, 128), 1)
    order = jnp.where(c == (r & 7) * GROUP + (r >> 3), 1.0, 0.0).astype(jnp.bfloat16)
    flow = jnp.concatenate([fx, fy, jnp.zeros((6, 128), jnp.float32)], 0)
    out = jnp.zeros((8, 128), jnp.float32)
    for _ in range(3):
        part = flow.astype(jnp.bfloat16)
        out = out + jnp.dot(part, order, preferred_element_type=jnp.float32)
        flow = flow - part.astype(jnp.float32)
    f_ref[...] = out[0:2]
    k = merged([cols[j] for j in range(NPIECE)], NPIECE)
    x, y = cell(sc[1] + iota((1, PIECE), 1))
    b_ref[0:1, :] = (k[1:2] / k[0:1] + (256.0 - x)) / FRAME_W
    b_ref[1:2, :] = (k[2:3] / k[0:1] - y) / FRAME_W


def coords(i):
    out = {}
    for name in reversed(AXES):
        out[name] = i % SIZES[name]
        i //= SIZES[name]
    return out


def swap(value, **flips):
    def partner(i):
        at = coords(i)
        for name, flip in flips.items():
            at[name] ^= flip
        return functools.reduce(lambda a, name: a * SIZES[name] + at[name], AXES, 0)

    return lax.ppermute(value, AXES, [(i, partner(i)) for i in range(256)])


def ring(value, step):
    def partner(i):
        at = coords(i)
        z = (at["zh"] * 2 + at["zl"] + step) % 8
        at["zh"], at["zl"] = z // 2, z % 2
        return functools.reduce(lambda a, name: a * SIZES[name] + at[name], AXES, 0)

    return lax.ppermute(value, AXES, [(i, partner(i)) for i in range(256)])


def vmem(count):
    return [pl.BlockSpec(memory_space=pltpu.VMEM)] * count


def on_device(q, k):
    me = {name: lax.axis_index(name) for name in AXES}
    z = me["zh"] * 2 + me["zl"]
    pieces, offsets = [k], [0]
    up = down = k
    for step in range(1, 5):
        up = ring(up, 1)
        pieces.append(up)
        offsets.append(-step)
        if step < 4:
            down = ring(down, -1)
            pieces.append(down)
            offsets.append(step)
    a = jnp.concatenate([q] + [swap(q, x=j) for j in (1, 2, 3)])
    b = jnp.concatenate([a] + [swap(a, y=j) for j in (1, 2, 3)])
    other = swap(b, core=1)

    origin = [(z + off) % 8 for off in offsets]
    bases = [
        (((o // 2) * 8 + me["x"] * 2 + me["core"]) * 8 + (o % 2) * 4 + me["y"]) * PIECE
        for o in origin
    ]
    zero = jnp.int32(0)
    sc = jnp.stack(
        [me["core"], me["y"] * 4 + me["x"], me["zl"], me["zh"], zero, zero, zero, zero]
        + bases + origin
    ).astype(jnp.int32)
    smem = pl.BlockSpec(memory_space=pltpu.SMEM)
    rows, cols = pl.pallas_call(
        main_kernel,
        name="match",
        out_shape=[
            jax.ShapeDtypeStruct((32, 4, 128), jnp.float32),
            jax.ShapeDtypeStruct((8, 4, PIECE), jnp.float32),
        ],
        in_specs=[smem] + vmem(2 + NPIECE),
        out_specs=vmem(2),
        scratch_shapes=[
            pltpu.VMEM((4096, CH), jnp.float32),
            pltpu.VMEM((4096, CH), jnp.bfloat16),
            pltpu.VMEM((NPIECE * PIECE, CH), jnp.bfloat16),
            pltpu.VMEM((3, 8, 4096), jnp.float32),
            pltpu.VMEM((PIECE, 128), jnp.float32),
            pltpu.VMEM((PIECE, 128), jnp.float32),
            pltpu.VMEM((8, 4096), jnp.float32),
            pltpu.VMEM((NPIECE * PIECE, 128), jnp.float32),
        ],
        compiler_params=pltpu.CompilerParams(vmem_limit_bytes=48 * 2**20),
    )(sc, b, other, *pieces)
    rows = lax.all_to_all(rows, ("core", "y", "x"), 0, 0)
    cols = lax.all_to_all(cols, ("zh", "zl"), 0, 0)
    shard_q = ((me["zl"] * 4 + me["y"]) * 4 + me["zh"]) * 8 + me["x"] * 2 + me["core"]
    own = jnp.stack([shard_q * 128, bases[0]]).astype(jnp.int32)
    return pl.pallas_call(
        final_kernel,
        name="finish",
        out_shape=[
            jax.ShapeDtypeStruct((2, 128), jnp.float32),
            jax.ShapeDtypeStruct((2, PIECE), jnp.float32),
        ],
        in_specs=[smem] + vmem(2),
        out_specs=vmem(2),
    )(own, rows, cols)


def solution(mesh):
    fine = Mesh(mesh.devices.reshape(tuple(SIZES[name] for name in AXES)), AXES)
    query = P(AXES)
    key = P(("zh", "x", "core", "zl", "y"))
    return jax.shard_map(
        on_device,
        mesh=fine,
        in_specs=(query, key),
        out_specs=(P(None, AXES), P(None, ("zh", "x", "core", "zl", "y"))),
        check_vma=False,
    )
```

```python
import functools
import math

import jax
import jax.numpy as jnp
from jax import lax
from jax.experimental import pallas as pl
from jax.experimental.pallas import tpu as pltpu
from jax.sharding import Mesh
from jax.sharding import PartitionSpec as P

FRAME_W = 480
CH = 128
BAND = 4096
PIECE = 512
RUN = 32
ORDER = (0, 1, 3, 2)
TILES = 4
SCALE = math.log2(math.e) / math.sqrt(CH)
LOW, HIGH = 2.0**-90, 2.0**100
AXES = ("zl", "y", "zh", "x", "core")
SIZES = {"zl": 2, "y": 4, "zh": 4, "x": 4, "core": 2}
NT = (((1,), (1,)), ((), ()))
CORE, X, Y, Z, PIECE_Z = 0, 1, 2, 3, 4


def nt_dot(a, b):
    return lax.dot_general(a, b, NT, preferred_element_type=jnp.float32)


def split2(v):
    high = v.astype(jnp.bfloat16)
    return high, (v - high.astype(jnp.float32)).astype(jnp.bfloat16)


def cell(n):
    y = ((n >> 5) * 4370) >> 16
    return (n - y * FRAME_W).astype(jnp.float32), y.astype(jnp.float32)


def iota(shape, axis):
    return lax.broadcasted_iota(jnp.int32, shape, axis)


def key_base(z, y, x, core):
    return ((((z >> 1) * 4 + x) * 2 + core) * 8 + (z & 1) * 4 + y) * 512


def query_base(z, y, x, core):
    return ((((z & 1) * 4 + y) * 4 + (z >> 1)) * 8 + x * 2 + core) * 128


def key_weights(sc):
    lane = iota((16, 256), 1)
    row = iota((16, 256), 0)
    on_sum = lane < 128
    s, g = (lane >> 4) & 7, lane & 15
    x, y = cell(key_base(sc[Z], sc[Y], s & 3, s >> 2) + g * RUN)
    x, y = x + (RUN - 256.0), y - 128.0
    value = jnp.where(row == 0, 1.0, jnp.where(row == 1, x, jnp.where(row == 2, y, 0.0)))
    value = jnp.where(on_sum, value, jnp.where(row == 1, -1.0, 0.0))
    return value.astype(jnp.bfloat16)


def query_weights(sc, z, half):
    r = iota((8, 128), 0)
    slot = jnp.where(r < 4, ORDER[2 * half], ORDER[2 * half + 1])
    x, y = cell(query_base(z, sc[Y] ^ slot, sc[X], sc[CORE]) + (r & 3) * RUN)
    return x + (RUN - 256.0), y


def run_order():
    r, c = iota((256, 256), 0), iota((256, 256), 1)
    return jnp.where(c == (r & 7) * RUN + (r >> 3), 1.0, 0.0).astype(jnp.bfloat16)


def set_keys(sc, ka, kb, kf, kp):
    for j in range(4):
        slot = sc[X] ^ ORDER[j]
        for core, ref in ((sc[CORE], ka), (1 - sc[CORE], kb)):
            at = pl.multiple_of((core * 4 + slot) * 512, 512)
            kf[pl.ds(at, 512), :] = ref[j * 512 : j * 512 + 512, :].astype(jnp.float32)

    def tile(t, carry):
        rows = [kf[pl.ds(s * 512 + t, 16, stride=RUN), :] for s in range(8)]
        at = pl.multiple_of(t * 128, 128)
        kp[pl.ds(at, 128), :] = jnp.concatenate(rows, 0).astype(jnp.bfloat16)
        return carry

    lax.fori_loop(0, RUN, tile, 0, unroll=4)


def set_queries(ref, qp):
    perm = run_order()
    for half in range(2):
        rows = slice(half * 256, half * 256 + 256)
        qp[rows, :] = jnp.dot(perm, ref[rows, :], preferred_element_type=jnp.float32).astype(
            jnp.bfloat16
        )


def in_order(refs, part):
    got = []
    for run in range(4 * part, 4 * part + 4):
        there = pl.ds((run // 8) * 256 + run % 8, RUN, stride=8)
        got.append(jnp.concatenate([ref[there, :] for ref in refs], 1))
    return split2(jnp.concatenate(got, 0))


def one_piece(sc, z, qp, kp, acc, sums_ref, moments_ref, store, tops=None):
    tiles = TILES if tops is None else 1
    sums_ref[...] = jnp.zeros_like(sums_ref)
    moments_ref[...] = jnp.zeros_like(moments_ref)
    weights = [query_weights(sc, z, half) for half in range(2)]

    def chunk(j, carry):
        at = pl.multiple_of(j * tiles * 128, tiles * 128)
        lanes = pl.ds(at, tiles * 128)
        for half in range(2):
            s = nt_dot(qp[half * 256 : half * 256 + 256, :], kp[lanes, :]) * SCALE
            if tops is None:
                for_query = for_key = jnp.exp2(s)
            else:
                for_query = jnp.exp2(s - tops[0][half * 256 : half * 256 + 256, :])
                for_key = jnp.exp2(s - tops[1][0:1, lanes])
            sums, moments = [None] * tiles, [None] * tiles
            for u in range(RUN):
                rows = slice(half * 256 + u * 8, half * 256 + u * 8 + 8)
                own_sum, own_moment = sums_ref[rows, :], moments_ref[rows, :]
                for i in range(tiles):
                    part = (slice(u * 8, u * 8 + 8), slice(i * 128, i * 128 + 128))
                    e = for_key[part]
                    sums[i] = e if u == 0 else sums[i] + e
                    moments[i] = sums[i] if u == 0 else moments[i] + sums[i]
                    own_sum = own_sum + for_query[part]
                    own_moment = own_moment + own_sum
                sums_ref[rows, :] = own_sum
                moments_ref[rows, :] = own_moment
            x, y = weights[half]
            for i in range(tiles):
                d = pl.ds(pl.multiple_of(at + i * 128, 128), 128)
                acc[0, :, d] += sums[i]
                acc[1, :, d] += sums[i] * x - moments[i]
                acc[2, :, d] += sums[i] * y
        return carry

    count = BAND // 128 // tiles
    lax.fori_loop(0, count, chunk, 0, unroll=4 if tops is None else 1)
    w = key_weights(sc)
    for slot in range(4):
        hi, lo = in_order((sums_ref, moments_ref), slot)
        got = nt_dot(w, hi) + nt_dot(w, lo)
        store(slot, slice(0, 3), got[0:3])


def spread_keys(col_ref, acc, top=None):
    lane = iota((8, 128), 1) >> 4
    for stat in range(4):
        if stat == 3 and top is None:
            col_ref[:, 3:4, :] = jnp.zeros((8, 1, 512), jnp.float32)
            continue
        for block in range(4):
            out = jnp.zeros((8, 128), jnp.float32)
            for t in range(8):
                d = slice((block * 8 + t) * 128, (block * 8 + t) * 128 + 128)
                value = top[0:1, d] if stat == 3 else jnp.sum(acc[stat, :, d], 0, keepdims=True)
                value = pltpu.roll(jnp.broadcast_to(value, (8, 128)), 0, 1, stride=16, stride_axis=0)
                out = jnp.where(lane == t, pltpu.roll(value, (t * 16 + 16) % 128, 1), out)
            for s in range(8):
                lanes = slice(block * 128, block * 128 + 128)
                col_ref[s, stat : stat + 1, lanes] = out[7 - s : 8 - s, :]


def first_kernel(sc, ka, kb, q, kp, acc, rows, kf, qp, sums_ref, moments_ref):
    set_keys(sc, ka, kb, kf, kp)
    acc[...] = jnp.zeros_like(acc)
    set_queries(q, qp)

    def store(slot, stats, value):
        rows[0, slot, stats, :] = value

    one_piece(sc, sc[PIECE_Z], qp, kp, acc, sums_ref, moments_ref, store)


def more_kernel(first, sc, kp, old, *refs):
    count = (len(refs) - 5) // 1
    qs, (acc, rows, qp, sums_ref, moments_ref) = refs[:count], refs[count:]
    acc[...] = old[...]
    for i, q in enumerate(qs):
        set_queries(q, qp)

        def store(slot, stats, value, i=i):
            rows[i, slot, stats, :] = value

        one_piece(sc, sc[PIECE_Z + first + i], qp, kp, acc, sums_ref, moments_ref, store)


def last_kernel(sc, kp, old, q, r0, r1, r2, r3, *refs):
    pieces, refs = refs[:8], refs[8:]
    row_ref, col_ref, acc, qp, sums_ref, moments_ref, rm, km, raw, sem = refs
    acc[...] = old[...]
    set_queries(q, qp)

    def place(piece, slot):
        return sc[PIECE_Z + piece] * 4 + (sc[Y] ^ ORDER[slot])

    def store(piece, slot, stats, value):
        row_ref[place(piece, slot), stats, :] = value

    one_piece(
        sc, sc[PIECE_Z + 7], qp, kp, acc, sums_ref, moments_ref, functools.partial(store, 7)
    )
    piece = 0
    for ref in (r0, r1, r2, r3):
        for i in range(ref.shape[0]):
            for slot in range(4):
                store(piece, slot, slice(0, 3), ref[i, slot, 0:3, :])
            piece += 1
    row_ref[:, 3:4, :] = jnp.zeros((32, 1, 128), jnp.float32)
    spread_keys(col_ref, acc)
    row_sums, col_sums = row_ref[:, 0, :], col_ref[:, 0, :]
    low = jnp.minimum(jnp.min(row_sums), jnp.min(col_sums))
    high = jnp.maximum(jnp.max(row_sums), jnp.max(col_sums))

    @pl.when(jnp.logical_not((low > LOW) & (high < HIGH)))
    def _():
        acc[...] = jnp.zeros_like(acc)
        km[...] = jnp.full_like(km, -jnp.inf)
        pick = jnp.where((iota((16, 128), 0) == 0) & (iota((16, 128), 1) == 0), 1.0, 0.0)
        pick = pick.astype(jnp.bfloat16)

        def fetch(piece):
            copy = pltpu.make_async_copy(pieces[piece], raw, sem)
            copy.start()
            copy.wait()
            set_queries(raw, qp)

        def block_top(half, t):
            lanes = pl.ds(pl.multiple_of(t * 128, 128), 128)
            s = nt_dot(qp[half * 256 : half * 256 + 256, :], kp[lanes, :]) * SCALE
            return lanes, s

        for piece in range(8):
            fetch(piece)

            def chunk(t, carry):
                for half in range(2):
                    lanes, s = block_top(half, t)
                    km[:, lanes] = jnp.maximum(km[:, lanes], jnp.max(s.reshape(RUN, 8, 128), 0))
                return carry

            lax.fori_loop(0, BAND // 128, chunk, 0)
        km[...] = jnp.broadcast_to(jnp.max(km[...], 0, keepdims=True), km.shape)
        for piece in range(8):
            fetch(piece)
            for half in range(2):

                def chunk(t, top, half=half):
                    return jnp.maximum(top, block_top(half, t)[1])

                top = jnp.full((256, 128), -jnp.inf, jnp.float32)
                top = lax.fori_loop(0, BAND // 128, chunk, top)
                hi, lo = split2(jnp.broadcast_to(jnp.max(top, 1, keepdims=True), (256, 128)))
                rm[half * 256 : half * 256 + 256, :] = hi.astype(jnp.float32) + lo.astype(
                    jnp.float32
                )
            for slot in range(4):
                hi, lo = in_order((rm,), slot)
                store(piece, slot, slice(3, 4), (nt_dot(pick, hi) + nt_dot(pick, lo))[0:1])
            one_piece(
                sc, sc[PIECE_Z + piece], qp, kp, acc, sums_ref, moments_ref,
                functools.partial(store, piece), (rm, km),
            )
        spread_keys(col_ref, acc, km)


def final_kernel(sc, rows, cols, f_ref, b_ref):
    def merged(parts):
        top = parts[0][3:4]
        for part in parts[1:]:
            top = jnp.maximum(top, part[3:4])
        return sum(part[0:3] * jnp.exp2(part[3:4] - top) for part in parts)

    q = merged([rows[j] for j in range(32)])
    x, y = cell(query_base(sc[Z], sc[Y], sc[X], sc[CORE]) + iota((1, 128), 1))
    f_ref[0:1, :] = (q[1:2] / q[0:1] + (256.0 - x)) / FRAME_W
    f_ref[1:2, :] = (q[2:3] / q[0:1] + (128.0 - y)) / FRAME_W
    k = merged([cols[j] for j in range(8)])
    lane = iota((1, 512), 1)
    x, y = cell(key_base(sc[Z], sc[Y], sc[X], sc[CORE]) + (lane & 15) * RUN + (lane >> 4))
    bx = (k[1:2] / k[0:1] + (256.0 - x)) / FRAME_W
    by = (k[2:3] / k[0:1] - y) / FRAME_W
    r, c = iota((512, 512), 0), iota((512, 512), 1)
    order = jnp.where(c == (r & 15) * RUN + (r >> 4), 1.0, 0.0).astype(jnp.bfloat16)
    flow = jnp.concatenate([bx, by, jnp.zeros((6, 512), jnp.float32)], 0)
    parts = []
    for _ in range(3):
        parts.append(flow.astype(jnp.bfloat16))
        flow = flow - parts[-1].astype(jnp.float32)
    out = jnp.dot(jnp.concatenate(parts, 0), order, preferred_element_type=jnp.float32)
    b_ref[...] = out[0:2] + out[8:10] + out[16:18]


def coords(i):
    out = {}
    for name in reversed(AXES):
        out[name] = i % SIZES[name]
        i //= SIZES[name]
    return out


def index(at):
    return functools.reduce(lambda a, name: a * SIZES[name] + at[name], AXES, 0)


def swap(value, **flips):
    def partner(i):
        at = coords(i)
        for name, flip in flips.items():
            at[name] ^= flip
        return index(at)

    return lax.ppermute(value, AXES, [(i, partner(i)) for i in range(256)])


def ring(value, step):
    def partner(i):
        at = coords(i)
        z = (at["zh"] * 2 + at["zl"] + step) % 8
        at["zh"], at["zl"] = z // 2, z % 2
        return index(at)

    return lax.ppermute(value, AXES, [(i, partner(i)) for i in range(256)])


SMEM = pl.BlockSpec(memory_space=pltpu.SMEM)
VMEM = pl.BlockSpec(memory_space=pltpu.VMEM)
ANY = pl.BlockSpec(memory_space=pl.ANY)


def f32(*shape):
    return jax.ShapeDtypeStruct(shape, jnp.float32)


def call(kernel, name, args, in_specs, out_shape, scratch, pieces, alias=None):
    return pl.pallas_call(
        kernel,
        name=name,
        out_shape=out_shape,
        in_specs=in_specs,
        out_specs=[VMEM] * len(out_shape),
        scratch_shapes=scratch,
        input_output_aliases=alias or {},
        cost_estimate=pl.CostEstimate(
            flops=pieces * 2 * PIECE * BAND * 256, bytes_accessed=2**21, transcendentals=pieces * PIECE * BAND
        ),
        compiler_params=pltpu.CompilerParams(vmem_limit_bytes=40 * 2**20),
    )(*args)


def on_device(q, k):
    me = {name: lax.axis_index(name) for name in AXES}
    z = me["zh"] * 2 + me["zl"]
    ka = jnp.concatenate([k] + [swap(k, x=j) for j in ORDER[1:]])
    own = jnp.concatenate([q] + [swap(q, y=j) for j in ORDER[1:]])
    kb = swap(ka, core=1)
    z_of = [(z + off) % 8 for off in (0, -1, 1, -2, 2, -3, 3, -4)]
    sc = jnp.stack([me["core"], me["x"], me["y"], z] + z_of).astype(jnp.int32)

    half_sums = [pltpu.VMEM((PIECE, 128), jnp.float32)] * 2
    piece_rows = pltpu.VMEM((PIECE, CH), jnp.bfloat16)
    pieces = [own, ring(own, 1), ring(own, -1)]
    kp, acc, r0 = call(
        first_kernel, "first", (sc, ka, kb, own), [SMEM, VMEM, VMEM, VMEM],
        [jax.ShapeDtypeStruct((BAND, CH), jnp.bfloat16), f32(3, 8, BAND), f32(1, 4, 4, 128)],
        [pltpu.VMEM((BAND, CH), jnp.float32), piece_rows] + half_sums, 1,
    )
    parts = [r0]
    for first in (1, 3, 5):
        up, down, acc = lax.optimization_barrier((pieces[first], pieces[first + 1], acc))
        pieces += [ring(up, 1), ring(down, -1)] if first < 5 else [ring(up, 1)]
        acc, got = call(
            functools.partial(more_kernel, first), f"more{first}",
            (sc, kp, acc, up, down), [SMEM] + [VMEM] * 4,
            [f32(3, 8, BAND), f32(2, 4, 4, 128)], [piece_rows] + half_sums, 2,
        )
        parts.append(got)
    rows, cols = call(
        last_kernel, "last", (sc, kp, acc, pieces[7], *parts, *pieces),
        [SMEM] + [VMEM] * 7 + [ANY] * 8, [f32(32, 4, 128), f32(8, 4, 512)],
        [pltpu.VMEM((3, 8, BAND), jnp.float32), piece_rows] + half_sums
        + [pltpu.VMEM((PIECE, 128), jnp.float32), pltpu.VMEM((8, BAND), jnp.float32),
           piece_rows, pltpu.SemaphoreType.DMA], 1,
    )
    rows = lax.all_to_all(rows, ("zh", "zl", "y"), 0, 0)
    cols = lax.all_to_all(cols, ("core", "x"), 0, 0)
    return call(
        final_kernel, "finish", (sc, rows, cols), [SMEM, VMEM, VMEM], [f32(2, 128), f32(2, 512)], [], 0
    )


def solution(mesh):
    fine = Mesh(mesh.devices.reshape(tuple(SIZES[name] for name in AXES)), AXES)
    key = ("zh", "x", "core", "zl", "y")
    return jax.shard_map(
        on_device,
        mesh=fine,
        in_specs=(P(AXES), P(key)),
        out_specs=(P(None, AXES), P(None, key)),
        check_vma=False,
    )
```

```python
import functools
import math

import jax
import jax.numpy as jnp
from jax import lax
from jax.experimental import pallas as pl
from jax.experimental.pallas import tpu as pltpu
from jax.sharding import Mesh
from jax.sharding import PartitionSpec as P

FRAME_W = 480
CH = 128
BAND = 4096
PIECE = 512
RUN = 32
TILES = 4
UNROLL = 4
SCALE = math.log2(math.e) / math.sqrt(CH)
LOW, HIGH = 2.0**-90, 2.0**100
AXES = ("zl", "y", "zh", "x", "core")
SIZES = {"zl": 2, "y": 4, "zh": 4, "x": 4, "core": 2}
NT = (((1,), (1,)), ((), ()))
CORE, X, Y, Z, PIECE_Z = 0, 1, 2, 3, 4


def nt_dot(a, b):
    return lax.dot_general(a, b, NT, preferred_element_type=jnp.float32)


def split2(v):
    high = v.astype(jnp.bfloat16)
    return high, (v - high.astype(jnp.float32)).astype(jnp.bfloat16)


def cell(n):
    y = ((n >> 5) * 4370) >> 16
    return (n - y * FRAME_W).astype(jnp.float32), y.astype(jnp.float32)


def iota(shape, axis):
    return lax.broadcasted_iota(jnp.int32, shape, axis)


def key_base(z, y, x, core):
    return ((((z >> 1) * 4 + x) * 2 + core) * 8 + (z & 1) * 4 + y) * 512


def query_base(z, y, x, core):
    return ((((z & 1) * 4 + y) * 4 + (z >> 1)) * 8 + x * 2 + core) * 128


def key_weights(sc):
    lane = iota((16, 256), 1)
    row = iota((16, 256), 0)
    on_sum = lane < 128
    s, g = (lane >> 4) & 7, lane & 15
    x, y = cell(key_base(sc[Z], sc[Y], s & 3, s >> 2) + g * RUN)
    x, y = x + (RUN - 256.0), y - 128.0
    value = jnp.where(row == 0, 1.0, jnp.where(row == 1, x, jnp.where(row == 2, y, 0.0)))
    value = jnp.where(on_sum, value, jnp.where(row == 1, -1.0, 0.0))
    return value.astype(jnp.bfloat16)


def query_weights(sc, z, half):
    r = iota((8, 128), 0)
    slot = jnp.where(r < 4, 2 * half, 2 * half + 1)
    x, y = cell(query_base(z, sc[Y] ^ slot, sc[X], sc[CORE]) + (r & 3) * RUN)
    return x + (RUN - 256.0), y


def run_order():
    r, c = iota((256, 256), 0), iota((256, 256), 1)
    return jnp.where(c == (r & 7) * RUN + (r >> 3), 1.0, 0.0).astype(jnp.bfloat16)


def set_keys(sc, ka, kb, kf, kp):
    for j in range(4):
        slot = sc[X] ^ j
        for core, ref in ((sc[CORE], ka), (1 - sc[CORE], kb)):
            at = pl.multiple_of((core * 4 + slot) * 512, 512)
            kf[pl.ds(at, 512), :] = ref[j * 512 : j * 512 + 512, :].astype(jnp.float32)

    def tile(t, carry):
        rows = [kf[pl.ds(s * 512 + t, 16, stride=RUN), :] for s in range(8)]
        at = pl.multiple_of(t * 128, 128)
        kp[pl.ds(at, 128), :] = jnp.concatenate(rows, 0).astype(jnp.bfloat16)
        return carry

    lax.fori_loop(0, RUN, tile, 0, unroll=4)


def set_queries(refs, qp):
    perm = run_order()
    for i, ref in enumerate(refs):
        for half in range(2):
            rows = slice(half * 256, half * 256 + 256)
            got = jnp.dot(perm, ref[rows, :], preferred_element_type=jnp.float32)
            qp[i * PIECE + half * 256 : i * PIECE + half * 256 + 256, :] = got.astype(jnp.bfloat16)


def in_order(refs, part):
    got = []
    for run in range(4 * part, 4 * part + 4):
        there = pl.ds((run // 8) * 256 + run % 8, RUN, stride=8)
        got.append(jnp.concatenate([ref[there, :] for ref in refs], 1))
    return split2(jnp.concatenate(got, 0))


def block(sc, zs, qp, kp, acc, sums_ref, moments_ref, store, tops=None):
    tiles = TILES if tops is None else 1
    halves = 2 * len(zs)
    sums_ref[...] = jnp.zeros_like(sums_ref)
    moments_ref[...] = jnp.zeros_like(moments_ref)
    weights = [query_weights(sc, zs[half // 2], half % 2) for half in range(halves)]

    def chunk(j, carry):
        at = pl.multiple_of(j * tiles * 128, tiles * 128)
        lanes = pl.ds(at, tiles * 128)
        s = nt_dot(qp[0 : halves * 256, :], kp[lanes, :]) * SCALE
        if tops is None:
            for_query = for_key = jnp.exp2(s)
        else:
            for_query = jnp.exp2(s - tops[0][...])
            for_key = jnp.exp2(s - tops[1][0:1, lanes])
        for half in range(halves):
            sums, moments = [None] * tiles, [None] * tiles
            for u in range(RUN):
                rows = slice(half * 256 + u * 8, half * 256 + u * 8 + 8)
                own_sum, own_moment = sums_ref[rows, :], moments_ref[rows, :]
                for i in range(tiles):
                    part = (rows, slice(i * 128, i * 128 + 128))
                    e = for_key[part]
                    sums[i] = e if u == 0 else sums[i] + e
                    moments[i] = sums[i] if u == 0 else moments[i] + sums[i]
                    own_sum = own_sum + for_query[part]
                    own_moment = own_moment + own_sum
                sums_ref[rows, :] = own_sum
                moments_ref[rows, :] = own_moment
            x, y = weights[half]
            for i in range(tiles):
                d = pl.ds(pl.multiple_of(at + i * 128, 128), 128)
                acc[0, :, d] += sums[i]
                acc[1, :, d] += sums[i] * x - moments[i]
                acc[2, :, d] += sums[i] * y
        return carry

    lax.fori_loop(0, BAND // 128 // tiles, chunk, 0, unroll=UNROLL if tops is None else 1)
    w = key_weights(sc)
    for piece in range(len(zs)):
        for slot in range(4):
            hi, lo = in_order((sums_ref, moments_ref), 4 * piece + slot)
            store(piece, slot, slice(0, 3), (nt_dot(w, hi) + nt_dot(w, lo))[0:3])


def spread_keys(sc, near, far, spread, acc, top=None):
    lane = iota((8, 128), 1) >> 4
    for stat in range(4):
        if stat == 3 and top is None:
            near[:, 3:4, :] = jnp.zeros((4, 1, 512), jnp.float32)
            far[:, 3:4, :] = jnp.zeros((4, 1, 512), jnp.float32)
            continue
        for part in range(4):
            out = jnp.zeros((8, 128), jnp.float32)
            for t in range(8):
                d = slice((part * 8 + t) * 128, (part * 8 + t) * 128 + 128)
                value = top[0:1, d] if stat == 3 else jnp.sum(acc[stat, :, d], 0, keepdims=True)
                value = pltpu.roll(jnp.broadcast_to(value, (8, 128)), 0, 1, stride=16, stride_axis=0)
                out = jnp.where(lane == t, pltpu.roll(value, (t * 16 + 16) % 128, 1), out)
            spread[:, part * 128 : part * 128 + 128] = out
        for i, ref in enumerate((near, far)):
            for j in range(4):
                row = 7 - ((sc[CORE] ^ i) * 4 + (sc[X] ^ j))
                ref[j, stat : stat + 1, :] = spread[pl.ds(row, 1), :]


def first_kernel(sc, ka, kb, q, kp, acc, rows, kf, qp, sums_ref, moments_ref):
    set_keys(sc, ka, kb, kf, kp)
    acc[...] = jnp.zeros_like(acc)
    set_queries([q], qp)

    def store(piece, slot, stats, value):
        rows[piece, slot, stats, :] = value

    block(sc, [sc[PIECE_Z]], qp, kp, acc, sums_ref, moments_ref, store)


def more_kernel(first, sc, kp, old, *refs):
    count = len(refs) - 5
    qs, (acc, rows, qp, sums_ref, moments_ref) = refs[:count], refs[count:]
    acc[...] = old[...]
    set_queries(qs, qp)

    def store(piece, slot, stats, value):
        rows[piece, slot, stats, :] = value

    zs = [sc[PIECE_Z + first + i] for i in range(count)]
    block(sc, zs, qp, kp, acc, sums_ref, moments_ref, store)


def last_kernel(sc, kp, old, q, r0, r1, r2, r3, *refs):
    pieces, refs = refs[:8], refs[8:]
    row_ref, near, far, acc, qp, sums_ref, moments_ref, spread, rm, km, raw, sem = refs
    acc[...] = old[...]
    set_queries([q], qp)

    def place(piece, slot):
        return sc[PIECE_Z + piece] * 4 + (sc[Y] ^ slot)

    def store(piece, slot, stats, value):
        row_ref[place(piece, slot), stats, :] = value

    block(
        sc, [sc[PIECE_Z + 7]], qp, kp, acc, sums_ref, moments_ref,
        lambda _, *what: store(7, *what),
    )
    piece = 0
    for ref in (r0, r1, r2, r3):
        for i in range(ref.shape[0]):
            for slot in range(4):
                store(piece, slot, slice(0, 3), ref[i, slot, 0:3, :])
            piece += 1
    row_ref[:, 3:4, :] = jnp.zeros((32, 1, 128), jnp.float32)
    spread_keys(sc, near, far, spread, acc)
    sums = [row_ref[:, 0, :], near[:, 0, :], far[:, 0, :]]
    low = functools.reduce(jnp.minimum, [jnp.min(v) for v in sums])
    high = functools.reduce(jnp.maximum, [jnp.max(v) for v in sums])

    @pl.when(jnp.logical_not((low > LOW) & (high < HIGH)))
    def _():
        acc[...] = jnp.zeros_like(acc)
        km[...] = jnp.full_like(km, -jnp.inf)
        pick = jnp.where((iota((16, 128), 0) == 0) & (iota((16, 128), 1) == 0), 1.0, 0.0)
        pick = pick.astype(jnp.bfloat16)

        def fetch(piece):
            copy = pltpu.make_async_copy(pieces[piece], raw, sem)
            copy.start()
            copy.wait()
            set_queries([raw], qp)

        def block_top(half, t):
            lanes = pl.ds(pl.multiple_of(t * 128, 128), 128)
            s = nt_dot(qp[half * 256 : half * 256 + 256, :], kp[lanes, :]) * SCALE
            return lanes, s

        for piece in range(8):
            fetch(piece)

            def chunk(t, carry):
                for half in range(2):
                    lanes, s = block_top(half, t)
                    km[:, lanes] = jnp.maximum(km[:, lanes], jnp.max(s.reshape(RUN, 8, 128), 0))
                return carry

            lax.fori_loop(0, BAND // 128, chunk, 0)
        km[...] = jnp.broadcast_to(jnp.max(km[...], 0, keepdims=True), km.shape)
        for piece in range(8):
            fetch(piece)
            for half in range(2):

                def chunk(t, top, half=half):
                    return jnp.maximum(top, block_top(half, t)[1])

                top = jnp.full((256, 128), -jnp.inf, jnp.float32)
                top = lax.fori_loop(0, BAND // 128, chunk, top)
                hi, lo = split2(jnp.broadcast_to(jnp.max(top, 1, keepdims=True), (256, 128)))
                rm[half * 256 : half * 256 + 256, :] = hi.astype(jnp.float32) + lo.astype(
                    jnp.float32
                )
            for slot in range(4):
                hi, lo = in_order((rm,), slot)
                store(piece, slot, slice(3, 4), (nt_dot(pick, hi) + nt_dot(pick, lo))[0:1])
            block(
                sc, [sc[PIECE_Z + piece]], qp, kp, acc, sums_ref, moments_ref,
                lambda _, *what, piece=piece: store(piece, *what), (rm, km),
            )
        spread_keys(sc, near, far, spread, acc, km)


def merged(parts):
    top = parts[0][3:4]
    for part in parts[1:]:
        top = jnp.maximum(top, part[3:4])
    return sum(part[0:3] * jnp.exp2(part[3:4] - top) for part in parts), top


def merge_kernel(a, b, *outs):
    for j, out in enumerate(outs):
        out[0:3, :], out[3:4, :] = merged([a[j], b[j]])


def final_kernel(sc, rows, k0, k1, k2, k3, f_ref, b_ref):
    q, _ = merged([rows[j] for j in range(32)])
    x, y = cell(query_base(sc[Z], sc[Y], sc[X], sc[CORE]) + iota((1, 128), 1))
    f_ref[0:1, :] = (q[1:2] / q[0:1] + (256.0 - x)) / FRAME_W
    f_ref[1:2, :] = (q[2:3] / q[0:1] + (128.0 - y)) / FRAME_W
    k, _ = merged([ref[...] for ref in (k0, k1, k2, k3)])
    lane = iota((1, 512), 1)
    x, y = cell(key_base(sc[Z], sc[Y], sc[X], sc[CORE]) + (lane & 15) * RUN + (lane >> 4))
    bx = (k[1:2] / k[0:1] + (256.0 - x)) / FRAME_W
    by = (k[2:3] / k[0:1] - y) / FRAME_W
    r, c = iota((512, 512), 0), iota((512, 512), 1)
    order = jnp.where(c == (r & 15) * RUN + (r >> 4), 1.0, 0.0).astype(jnp.bfloat16)
    flow = jnp.concatenate([bx, by, jnp.zeros((6, 512), jnp.float32)], 0)
    parts = []
    for _ in range(3):
        parts.append(flow.astype(jnp.bfloat16))
        flow = flow - parts[-1].astype(jnp.float32)
    out = jnp.dot(jnp.concatenate(parts, 0), order, preferred_element_type=jnp.float32)
    b_ref[...] = out[0:2] + out[8:10] + out[16:18]


def coords(i):
    out = {}
    for name in reversed(AXES):
        out[name] = i % SIZES[name]
        i //= SIZES[name]
    return out


def index(at):
    return functools.reduce(lambda a, name: a * SIZES[name] + at[name], AXES, 0)


def swap(value, **flips):
    def partner(i):
        at = coords(i)
        for name, flip in flips.items():
            at[name] ^= flip
        return index(at)

    return lax.ppermute(value, AXES, [(i, partner(i)) for i in range(256)])


def ring(value, step):
    def partner(i):
        at = coords(i)
        z = (at["zh"] * 2 + at["zl"] + step) % 8
        at["zh"], at["zl"] = z // 2, z % 2
        return index(at)

    return lax.ppermute(value, AXES, [(i, partner(i)) for i in range(256)])


SMEM = pl.BlockSpec(memory_space=pltpu.SMEM)
VMEM = pl.BlockSpec(memory_space=pltpu.VMEM)
ANY = pl.BlockSpec(memory_space=pl.ANY)


def f32(*shape):
    return jax.ShapeDtypeStruct(shape, jnp.float32)


def call(kernel, name, args, in_specs, out_shape, scratch, pieces, alias=None):
    return pl.pallas_call(
        kernel,
        name=name,
        out_shape=out_shape,
        in_specs=in_specs,
        out_specs=[VMEM] * len(out_shape),
        scratch_shapes=scratch,
        input_output_aliases=alias or {},
        cost_estimate=pl.CostEstimate(
            flops=pieces * 2 * PIECE * BAND * 256, bytes_accessed=2**21, transcendentals=pieces * PIECE * BAND
        ),
        compiler_params=pltpu.CompilerParams(vmem_limit_bytes=40 * 2**20),
    )(*args)


def on_device(q, k):
    me = {name: lax.axis_index(name) for name in AXES}
    z = me["zh"] * 2 + me["zl"]
    by_y = [swap(q, y=j) for j in (1, 3, 2)]
    by_x = [swap(k, x=j) for j in (1, 3, 2)]
    by_y, by_x = lax.optimization_barrier((by_y, by_x))
    own = jnp.concatenate([q, by_y[0], by_y[2], by_y[1]])
    ka = jnp.concatenate([k, by_x[0], by_x[2], by_x[1]])
    kb = swap(ka, core=1)
    z_of = [(z + off) % 8 for off in (0, -1, 1, -2, 2, -3, 3, -4)]
    sc = jnp.stack([me["core"], me["x"], me["y"], z] + z_of).astype(jnp.int32)

    half_sums = [pltpu.VMEM((PIECE, 128), jnp.float32)] * 2
    piece_rows = pltpu.VMEM((PIECE, CH), jnp.bfloat16)
    two = [pltpu.VMEM((2 * PIECE, CH), jnp.bfloat16)] + [pltpu.VMEM((2 * PIECE, 128), jnp.float32)] * 2
    pieces = [own, ring(own, 1), ring(own, -1)]
    kp, acc, r0 = call(
        first_kernel, "first", (sc, ka, kb, own), [SMEM, VMEM, VMEM, VMEM],
        [jax.ShapeDtypeStruct((BAND, CH), jnp.bfloat16), f32(3, 8, BAND), f32(1, 4, 4, 128)],
        [pltpu.VMEM((BAND, CH), jnp.float32), piece_rows] + half_sums, 1,
    )
    parts = [r0]
    for first in (1, 3, 5):
        up, down, acc = lax.optimization_barrier((pieces[first], pieces[first + 1], acc))
        pieces += [ring(up, 1), ring(down, -1)] if first < 5 else [ring(up, 1)]
        acc, got = call(
            functools.partial(more_kernel, first), f"more{first}",
            (sc, kp, acc, up, down), [SMEM] + [VMEM] * 4,
            [f32(3, 8, BAND), f32(2, 4, 4, 128)], two, 2,
        )
        parts.append(got)
    rows, near, far = call(
        last_kernel, "last", (sc, kp, acc, pieces[7], *parts, *pieces),
        [SMEM] + [VMEM] * 7 + [ANY] * 8, [f32(32, 4, 128), f32(4, 4, 512), f32(4, 4, 512)],
        [pltpu.VMEM((3, 8, BAND), jnp.float32), piece_rows] + half_sums
        + [pltpu.VMEM((8, 512), jnp.float32), pltpu.VMEM((PIECE, 128), jnp.float32),
           pltpu.VMEM((8, BAND), jnp.float32), piece_rows, pltpu.SemaphoreType.DMA], 1,
    )
    cols = call(
        merge_kernel, "merge", (near, swap(far, core=1)), [VMEM] * 2, [f32(4, 512)] * 4, [], 0
    )
    cols = [cols[0]] + [swap(cols[j], x=j) for j in (1, 3, 2)]
    rows = lax.all_to_all(rows, ("zh", "zl", "y"), 0, 0)
    return call(
        final_kernel, "finish", (sc, rows, *cols), [SMEM] + [VMEM] * 5, [f32(2, 128), f32(2, 512)], [], 0
    )


def solution(mesh):
    fine = Mesh(mesh.devices.reshape(tuple(SIZES[name] for name in AXES)), AXES)
    key = ("zh", "x", "core", "zl", "y")
    return jax.shard_map(
        on_device,
        mesh=fine,
        in_specs=(P(AXES), P(key)),
        out_specs=(P(None, AXES), P(None, key)),
        check_vma=False,
    )
```

```python
import functools
import math

import jax
import jax.numpy as jnp
from jax import lax
from jax.experimental import pallas as pl
from jax.experimental.pallas import tpu as pltpu
from jax.sharding import Mesh
from jax.sharding import PartitionSpec as P

FRAME_W = 480
CH = 128
BAND = 4096
PIECE = 512
RUN = 32
TILES = 4
UNROLL = 8
SCALE = math.log2(math.e) / math.sqrt(CH)
LOW, HIGH = 2.0**-90, 2.0**100
AXES = ("zl", "y", "zh", "x", "core")
SIZES = {"zl": 2, "y": 4, "zh": 4, "x": 4, "core": 2}
NT = (((1,), (1,)), ((), ()))
CORE, X, Y, Z, PIECE_Z = 0, 1, 2, 3, 4


def nt_dot(a, b):
    return lax.dot_general(a, b, NT, preferred_element_type=jnp.float32)


def split2(v):
    high = v.astype(jnp.bfloat16)
    return high, (v - high.astype(jnp.float32)).astype(jnp.bfloat16)


def cell(n):
    y = ((n >> 5) * 4370) >> 16
    return (n - y * FRAME_W).astype(jnp.float32), y.astype(jnp.float32)


def iota(shape, axis):
    return lax.broadcasted_iota(jnp.int32, shape, axis)


def key_base(z, y, x, core):
    return ((((z >> 1) * 4 + x) * 2 + core) * 8 + (z & 1) * 4 + y) * 512


def query_base(z, y, x, core):
    return ((((z & 1) * 4 + y) * 4 + (z >> 1)) * 8 + x * 2 + core) * 128


def key_weights(sc):
    lane = iota((16, 256), 1)
    row = iota((16, 256), 0)
    on_sum = lane < 128
    s, g = (lane >> 4) & 7, lane & 15
    x, y = cell(key_base(sc[Z], sc[Y], s & 3, s >> 2) + g * RUN)
    x, y = x + (RUN - 256.0), y - 128.0
    value = jnp.where(row == 0, 1.0, jnp.where(row == 1, x, jnp.where(row == 2, y, 0.0)))
    value = jnp.where(on_sum, value, jnp.where(row == 1, -1.0, 0.0))
    return value.astype(jnp.bfloat16)


def query_weights(sc, z, half):
    r = iota((8, 128), 0)
    slot = jnp.where(r < 4, 2 * half, 2 * half + 1)
    x, y = cell(query_base(z, sc[Y] ^ slot, sc[X], sc[CORE]) + (r & 3) * RUN)
    return x + (RUN - 256.0), y


def run_order():
    r, c = iota((256, 256), 0), iota((256, 256), 1)
    return jnp.where(c == (r & 7) * RUN + (r >> 3), 1.0, 0.0).astype(jnp.bfloat16)


def set_keys(sc, ka, kb, kp):
    perm = run_order()
    for core, ref in ((sc[CORE], ka), (1 - sc[CORE], kb)):
        for j in range(4):
            shard = core * 4 + (sc[X] ^ j)
            low, high = (
                jnp.dot(perm, ref[at : at + 256, :], preferred_element_type=jnp.float32)
                for at in (j * 512, j * 512 + 256)
            )
            for t in range(RUN):
                rows = jnp.concatenate([low[t * 8 : t * 8 + 8], high[t * 8 : t * 8 + 8]], 0)
                at = pl.multiple_of(t * 128 + shard * 16, 16)
                kp[pl.ds(at, 16), :] = rows.astype(jnp.bfloat16)


def set_queries(refs, qp):
    perm = run_order()
    for i, ref in enumerate(refs):
        for half in range(2):
            rows = slice(half * 256, half * 256 + 256)
            got = jnp.dot(perm, ref[rows, :], preferred_element_type=jnp.float32)
            qp[i * PIECE + half * 256 : i * PIECE + half * 256 + 256, :] = got.astype(jnp.bfloat16)


def in_order(refs, part):
    got = []
    for run in range(4 * part, 4 * part + 4):
        there = pl.ds((run // 8) * 256 + run % 8, RUN, stride=8)
        got.append(jnp.concatenate([ref[there, :] for ref in refs], 1))
    return split2(jnp.concatenate(got, 0))


def block(sc, zs, qp, kp, acc, sums_ref, moments_ref, store, tops=None):
    tiles = TILES if tops is None else 1
    halves = 2 * len(zs)
    sums_ref[...] = jnp.zeros_like(sums_ref)
    moments_ref[...] = jnp.zeros_like(moments_ref)
    weights = [query_weights(sc, zs[half // 2], half % 2) for half in range(halves)]

    def chunk(j, carry):
        at = pl.multiple_of(j * tiles * 128, tiles * 128)
        lanes = pl.ds(at, tiles * 128)
        s = nt_dot(qp[0 : halves * 256, :], kp[lanes, :]) * SCALE
        if tops is None:
            for_query = for_key = jnp.exp2(s)
        else:
            for_query = jnp.exp2(s - tops[0][...])
            for_key = jnp.exp2(s - tops[1][0:1, lanes])
        for half in range(halves):
            sums, moments = [None] * tiles, [None] * tiles
            for u in range(RUN):
                rows = slice(half * 256 + u * 8, half * 256 + u * 8 + 8)
                own_sum, own_moment = sums_ref[rows, :], moments_ref[rows, :]
                for i in range(tiles):
                    part = (rows, slice(i * 128, i * 128 + 128))
                    e = for_key[part]
                    sums[i] = e if u == 0 else sums[i] + e
                    moments[i] = sums[i] if u == 0 else moments[i] + sums[i]
                    own_sum = own_sum + for_query[part]
                    own_moment = own_moment + own_sum
                sums_ref[rows, :] = own_sum
                moments_ref[rows, :] = own_moment
            x, y = weights[half]
            for i in range(tiles):
                d = pl.ds(pl.multiple_of(at + i * 128, 128), 128)
                acc[0, :, d] += sums[i]
                acc[1, :, d] += sums[i] * x - moments[i]
                acc[2, :, d] += sums[i] * y
        return carry

    lax.fori_loop(0, BAND // 128 // tiles, chunk, 0, unroll=UNROLL if tops is None else 1)
    w = key_weights(sc)
    for piece in range(len(zs)):
        for slot in range(4):
            hi, lo = in_order((sums_ref, moments_ref), 4 * piece + slot)
            store(piece, slot, slice(0, 3), (nt_dot(w, hi) + nt_dot(w, lo))[0:3])


def spread_keys(sc, near, far, spread, acc, top=None):
    lane = iota((8, 128), 1) >> 4
    for stat in range(4):
        if stat == 3 and top is None:
            near[:, 3:4, :] = jnp.zeros((4, 1, 512), jnp.float32)
            far[:, 3:4, :] = jnp.zeros((4, 1, 512), jnp.float32)
            continue
        for part in range(4):
            out = jnp.zeros((8, 128), jnp.float32)
            for t in range(8):
                d = slice((part * 8 + t) * 128, (part * 8 + t) * 128 + 128)
                value = top[0:1, d] if stat == 3 else jnp.sum(acc[stat, :, d], 0, keepdims=True)
                value = pltpu.roll(jnp.broadcast_to(value, (8, 128)), 0, 1, stride=16, stride_axis=0)
                out = jnp.where(lane == t, pltpu.roll(value, (t * 16 + 16) % 128, 1), out)
            spread[:, part * 128 : part * 128 + 128] = out
        for i, ref in enumerate((near, far)):
            for j in range(4):
                row = 7 - ((sc[CORE] ^ i) * 4 + (sc[X] ^ j))
                ref[j, stat : stat + 1, :] = spread[pl.ds(row, 1), :]


def first_kernel(sc, ka, kb, q, kp, acc, rows, qp, sums_ref, moments_ref):
    set_keys(sc, ka, kb, kp)
    acc[...] = jnp.zeros_like(acc)
    set_queries([q], qp)

    def store(piece, slot, stats, value):
        rows[piece, slot, stats, :] = value

    block(sc, [sc[PIECE_Z]], qp, kp, acc, sums_ref, moments_ref, store)


def more_kernel(first, sc, kp, old, *refs):
    count = len(refs) - 5
    qs, (acc, rows, qp, sums_ref, moments_ref) = refs[:count], refs[count:]
    acc[...] = old[...]
    set_queries(qs, qp)

    def store(piece, slot, stats, value):
        rows[piece, slot, stats, :] = value

    zs = [sc[PIECE_Z + first + i] for i in range(count)]
    block(sc, zs, qp, kp, acc, sums_ref, moments_ref, store)


def last_kernel(sc, kp, old, q, r0, r1, r2, r3, *refs):
    pieces, refs = refs[:8], refs[8:]
    row_ref, near, far, acc, qp, sums_ref, moments_ref, spread, rm, km, raw, sem = refs
    acc[...] = old[...]
    set_queries([q], qp)

    def place(piece, slot):
        return sc[PIECE_Z + piece] * 4 + (sc[Y] ^ slot)

    def store(piece, slot, stats, value):
        row_ref[place(piece, slot), stats, :] = value

    block(
        sc, [sc[PIECE_Z + 7]], qp, kp, acc, sums_ref, moments_ref,
        lambda _, *what: store(7, *what),
    )
    piece = 0
    for ref in (r0, r1, r2, r3):
        for i in range(ref.shape[0]):
            for slot in range(4):
                store(piece, slot, slice(0, 3), ref[i, slot, 0:3, :])
            piece += 1
    row_ref[:, 3:4, :] = jnp.zeros((32, 1, 128), jnp.float32)
    spread_keys(sc, near, far, spread, acc)
    sums = [row_ref[:, 0, :], near[:, 0, :], far[:, 0, :]]
    low = functools.reduce(jnp.minimum, [jnp.min(v) for v in sums])
    high = functools.reduce(jnp.maximum, [jnp.max(v) for v in sums])

    @pl.when(jnp.logical_not((low > LOW) & (high < HIGH)))
    def _():
        acc[...] = jnp.zeros_like(acc)
        km[...] = jnp.full_like(km, -jnp.inf)
        pick = jnp.where((iota((16, 128), 0) == 0) & (iota((16, 128), 1) == 0), 1.0, 0.0)
        pick = pick.astype(jnp.bfloat16)

        def fetch(piece):
            copy = pltpu.make_async_copy(pieces[piece], raw, sem)
            copy.start()
            copy.wait()
            set_queries([raw], qp)

        def block_top(half, t):
            lanes = pl.ds(pl.multiple_of(t * 128, 128), 128)
            s = nt_dot(qp[half * 256 : half * 256 + 256, :], kp[lanes, :]) * SCALE
            return lanes, s

        for piece in range(8):
            fetch(piece)

            def chunk(t, carry):
                for half in range(2):
                    lanes, s = block_top(half, t)
                    km[:, lanes] = jnp.maximum(km[:, lanes], jnp.max(s.reshape(RUN, 8, 128), 0))
                return carry

            lax.fori_loop(0, BAND // 128, chunk, 0)
        km[...] = jnp.broadcast_to(jnp.max(km[...], 0, keepdims=True), km.shape)
        for piece in range(8):
            fetch(piece)
            for half in range(2):

                def chunk(t, top, half=half):
                    return jnp.maximum(top, block_top(half, t)[1])

                top = jnp.full((256, 128), -jnp.inf, jnp.float32)
                top = lax.fori_loop(0, BAND // 128, chunk, top)
                hi, lo = split2(jnp.broadcast_to(jnp.max(top, 1, keepdims=True), (256, 128)))
                rm[half * 256 : half * 256 + 256, :] = hi.astype(jnp.float32) + lo.astype(
                    jnp.float32
                )
            for slot in range(4):
                hi, lo = in_order((rm,), slot)
                store(piece, slot, slice(3, 4), (nt_dot(pick, hi) + nt_dot(pick, lo))[0:1])
            block(
                sc, [sc[PIECE_Z + piece]], qp, kp, acc, sums_ref, moments_ref,
                lambda _, *what, piece=piece: store(piece, *what), (rm, km),
            )
        spread_keys(sc, near, far, spread, acc, km)


def merged(parts):
    top = parts[0][3:4]
    for part in parts[1:]:
        top = jnp.maximum(top, part[3:4])
    return sum(part[0:3] * jnp.exp2(part[3:4] - top) for part in parts), top


def merge_kernel(a, b, *outs):
    r, c = iota((512, 512), 0), iota((512, 512), 1)
    order = jnp.where(c == (r & 15) * RUN + (r >> 4), 1.0, 0.0).astype(jnp.bfloat16)
    rows = []
    for j in range(4):
        rows += list(merged([a[j], b[j]]))
    left = jnp.concatenate(rows, 0)
    parts = []
    for _ in range(3):
        parts.append(left.astype(jnp.bfloat16))
        left = left - parts[-1].astype(jnp.float32)
    got = jnp.dot(jnp.concatenate(parts, 0), order, preferred_element_type=jnp.float32)
    got = got[0:16] + got[16:32] + got[32:48]
    for j, out in enumerate(outs):
        out[...] = got[4 * j : 4 * j + 4]


def final_kernel(sc, rows, k0, k1, k2, k3, f_ref, b_ref):
    q, _ = merged([rows[j] for j in range(32)])
    x, y = cell(query_base(sc[Z], sc[Y], sc[X], sc[CORE]) + iota((1, 128), 1))
    f_ref[0:1, :] = (q[1:2] / q[0:1] + (256.0 - x)) / FRAME_W
    f_ref[1:2, :] = (q[2:3] / q[0:1] + (128.0 - y)) / FRAME_W
    k, _ = merged([ref[...] for ref in (k0, k1, k2, k3)])
    x, y = cell(key_base(sc[Z], sc[Y], sc[X], sc[CORE]) + iota((1, 512), 1))
    b_ref[0:1, :] = (k[1:2] / k[0:1] + (256.0 - x)) / FRAME_W
    b_ref[1:2, :] = (k[2:3] / k[0:1] - y) / FRAME_W


def coords(i):
    out = {}
    for name in reversed(AXES):
        out[name] = i % SIZES[name]
        i //= SIZES[name]
    return out


def index(at):
    return functools.reduce(lambda a, name: a * SIZES[name] + at[name], AXES, 0)


def swap(value, **flips):
    def partner(i):
        at = coords(i)
        for name, flip in flips.items():
            at[name] ^= flip
        return index(at)

    return lax.ppermute(value, AXES, [(i, partner(i)) for i in range(256)])


def ring(value, odd):
    def partner(i):
        at = coords(i)
        z = (((at["zh"] * 2 + at["zl"] + odd) ^ 1) - odd) % 8
        at["zh"], at["zl"] = z // 2, z % 2
        return index(at)

    return lax.ppermute(value, AXES, [(i, partner(i)) for i in range(256)])


SMEM = pl.BlockSpec(memory_space=pltpu.SMEM)
VMEM = pl.BlockSpec(memory_space=pltpu.VMEM)
ANY = pl.BlockSpec(memory_space=pl.ANY)


def f32(*shape):
    return jax.ShapeDtypeStruct(shape, jnp.float32)


def call(kernel, name, args, in_specs, out_shape, scratch, pieces, alias=None):
    return pl.pallas_call(
        kernel,
        name=name,
        out_shape=out_shape,
        in_specs=in_specs,
        out_specs=[VMEM] * len(out_shape),
        scratch_shapes=scratch,
        input_output_aliases=alias or {},
        cost_estimate=pl.CostEstimate(
            flops=pieces * 2 * PIECE * BAND * 256, bytes_accessed=2**21, transcendentals=pieces * PIECE * BAND
        ),
        compiler_params=pltpu.CompilerParams(vmem_limit_bytes=40 * 2**20),
    )(*args)


def on_device(q, k):
    me = {name: lax.axis_index(name) for name in AXES}
    z = me["zh"] * 2 + me["zl"]
    by_y = [swap(q, y=j) for j in (1, 3, 2)]
    by_x = [swap(k, x=j) for j in (1, 3, 2)]
    by_y, by_x = lax.optimization_barrier((by_y, by_x))
    own = jnp.concatenate([q, by_y[0], by_y[2], by_y[1]])
    ka = jnp.concatenate([k, by_x[0], by_x[2], by_x[1]])
    kb = swap(ka, core=1)
    ahead = 1 - 2 * (z & 1)
    z_of = [(z + off * ahead) % 8 for off in (0, 1, -1, 2, -2, 3, -3, 4)]
    sc = jnp.stack([me["core"], me["x"], me["y"], z] + z_of).astype(jnp.int32)

    half_sums = [pltpu.VMEM((PIECE, 128), jnp.float32)] * 2
    piece_rows = pltpu.VMEM((PIECE, CH), jnp.bfloat16)
    two = [pltpu.VMEM((2 * PIECE, CH), jnp.bfloat16)] + [pltpu.VMEM((2 * PIECE, 128), jnp.float32)] * 2
    pieces = [own, ring(own, 0), ring(own, 1)]
    kp, acc, r0 = call(
        first_kernel, "first", (sc, ka, kb, own), [SMEM, VMEM, VMEM, VMEM],
        [jax.ShapeDtypeStruct((BAND, CH), jnp.bfloat16), f32(3, 8, BAND), f32(1, 4, 4, 128)],
        [piece_rows] + half_sums, 1,
    )
    parts = [r0]
    for first in (1, 3, 5):
        up, down, acc = lax.optimization_barrier((pieces[first], pieces[first + 1], acc))
        pieces += [ring(down, 0), ring(up, 1)] if first < 5 else [ring(down, 0)]
        acc, got = call(
            functools.partial(more_kernel, first), f"more{first}",
            (sc, kp, acc, up, down), [SMEM] + [VMEM] * 4,
            [f32(3, 8, BAND), f32(2, 4, 4, 128)], two, 2,
        )
        parts.append(got)
    rows, near, far = call(
        last_kernel, "last", (sc, kp, acc, pieces[7], *parts, *pieces),
        [SMEM] + [VMEM] * 7 + [ANY] * 8, [f32(32, 4, 128), f32(4, 4, 512), f32(4, 4, 512)],
        [pltpu.VMEM((3, 8, BAND), jnp.float32), piece_rows] + half_sums
        + [pltpu.VMEM((8, 512), jnp.float32), pltpu.VMEM((PIECE, 128), jnp.float32),
           pltpu.VMEM((8, BAND), jnp.float32), piece_rows, pltpu.SemaphoreType.DMA], 1,
    )
    cols = call(
        merge_kernel, "merge", (near, swap(far, core=1)), [VMEM] * 2, [f32(4, 512)] * 4, [], 0
    )
    cols = [cols[0]] + [swap(cols[j], x=j) for j in (1, 3, 2)]
    rows = lax.all_to_all(rows, ("zh", "zl", "y"), 0, 0)
    return call(
        final_kernel, "finish", (sc, rows, *cols), [SMEM] + [VMEM] * 5, [f32(2, 128), f32(2, 512)], [], 0
    )


def solution(mesh):
    fine = Mesh(mesh.devices.reshape(tuple(SIZES[name] for name in AXES)), AXES)
    key = ("zh", "x", "core", "zl", "y")
    return jax.shard_map(
        on_device,
        mesh=fine,
        in_specs=(P(AXES), P(key)),
        out_specs=(P(None, AXES), P(None, key)),
        check_vma=False,
    )
```

```python
import functools
import math

import jax
import jax.numpy as jnp
from jax import lax
from jax.experimental import pallas as pl
from jax.experimental.pallas import tpu as pltpu
from jax.sharding import Mesh
from jax.sharding import PartitionSpec as P

FRAME_W = 480
CH = 128
BAND = 4096
PIECE = 512
RUN = 32
TILES = 4
UNROLL = 8
SCALE = math.log2(math.e) / math.sqrt(CH)
LOW, HIGH = 2.0**-90, 2.0**100
AXES = ("zl", "y", "zh", "x", "core")
SIZES = {"zl": 2, "y": 4, "zh": 4, "x": 4, "core": 2}
NT = (((1,), (1,)), ((), ()))
CORE, X, Y, Z, PIECE_Z = 0, 1, 2, 3, 4


def nt_dot(a, b):
    return lax.dot_general(a, b, NT, preferred_element_type=jnp.float32)


def split2(v):
    high = v.astype(jnp.bfloat16)
    return high, (v - high.astype(jnp.float32)).astype(jnp.bfloat16)


def cell(n):
    y = ((n >> 5) * 4370) >> 16
    return (n - y * FRAME_W).astype(jnp.float32), y.astype(jnp.float32)


def iota(shape, axis):
    return lax.broadcasted_iota(jnp.int32, shape, axis)


def key_base(z, y, x, core):
    return ((((z >> 1) * 4 + x) * 2 + core) * 8 + (z & 1) * 4 + y) * 512


def query_base(z, y, x, core):
    return ((((z & 1) * 4 + y) * 4 + (z >> 1)) * 8 + x * 2 + core) * 128


def key_weights(sc):
    lane = iota((16, 256), 1)
    row = iota((16, 256), 0)
    on_sum = lane < 128
    s, g = (lane >> 4) & 7, lane & 15
    x, y = cell(key_base(sc[Z], sc[Y], s & 3, s >> 2) + g * RUN)
    x, y = x + (RUN - 256.0), y - 128.0
    value = jnp.where(row == 0, 1.0, jnp.where(row == 1, x, jnp.where(row == 2, y, 0.0)))
    value = jnp.where(on_sum, value, jnp.where(row == 1, -1.0, 0.0))
    return value.astype(jnp.bfloat16)


def query_weights(sc, z, half):
    r = iota((8, 128), 0)
    slot = jnp.where(r < 4, 2 * half, 2 * half + 1)
    x, y = cell(query_base(z, sc[Y] ^ slot, sc[X], sc[CORE]) + (r & 3) * RUN)
    return x + (RUN - 256.0), y


def run_order():
    r, c = iota((256, 256), 0), iota((256, 256), 1)
    return jnp.where(c == (r & 7) * RUN + (r >> 3), 1.0, 0.0).astype(jnp.bfloat16)


def set_keys(sc, ka, kb, kp):
    perm = run_order()
    for core, ref in ((sc[CORE], ka), (1 - sc[CORE], kb)):
        for j in range(4):
            shard = core * 4 + (sc[X] ^ j)
            low, high = (
                jnp.dot(perm, ref[at : at + 256, :], preferred_element_type=jnp.float32)
                for at in (j * 512, j * 512 + 256)
            )
            for t in range(RUN):
                rows = jnp.concatenate([low[t * 8 : t * 8 + 8], high[t * 8 : t * 8 + 8]], 0)
                at = pl.multiple_of(t * 128 + shard * 16, 16)
                kp[pl.ds(at, 16), :] = rows.astype(jnp.bfloat16)


def set_queries(refs, qp, plain=False):
    perm = run_order()
    for i, ref in enumerate(refs):
        for half in range(2):
            rows = slice(half * 256, half * 256 + 256)
            got = jnp.dot(perm, ref[rows, :], preferred_element_type=jnp.float32)
            to = slice(i * PIECE + half * 256, i * PIECE + half * 256 + 256)
            if plain:
                qp[to, :] = got.astype(jnp.bfloat16)
            else:
                qp[to, 0:CH], qp[to, CH : 2 * CH] = split2(got * SCALE)


def in_order(refs, part):
    got = []
    for run in range(4 * part, 4 * part + 4):
        there = pl.ds((run // 8) * 256 + run % 8, RUN, stride=8)
        got.append(jnp.concatenate([ref[there, :] for ref in refs], 1))
    return split2(jnp.concatenate(got, 0))


def block(sc, zs, qp, kp, acc, sums_ref, moments_ref, store, tops=None):
    tiles = TILES if tops is None else 1
    halves = 2 * len(zs)
    sums_ref[...] = jnp.zeros_like(sums_ref)
    moments_ref[...] = jnp.zeros_like(moments_ref)
    weights = [query_weights(sc, zs[half // 2], half % 2) for half in range(halves)]

    def chunk(j, carry):
        at = pl.multiple_of(j * tiles * 128, tiles * 128)
        lanes = pl.ds(at, tiles * 128)
        if tops is None:
            keys = kp[lanes, :]
            s = nt_dot(qp[0 : halves * 256, :], jnp.concatenate([keys, keys], 1))
            for_query = for_key = jnp.exp2(s)
        else:
            s = nt_dot(qp[...], kp[lanes, :]) * SCALE
            for_query = jnp.exp2(s - tops[0][...])
            for_key = jnp.exp2(s - tops[1][0:1, lanes])
        for half in range(halves):
            sums, moments = [None] * tiles, [None] * tiles
            for u in range(RUN):
                rows = slice(half * 256 + u * 8, half * 256 + u * 8 + 8)
                own_sum, own_moment = sums_ref[rows, :], moments_ref[rows, :]
                for i in range(tiles):
                    part = (rows, slice(i * 128, i * 128 + 128))
                    e = for_key[part]
                    sums[i] = e if u == 0 else sums[i] + e
                    moments[i] = sums[i] if u == 0 else moments[i] + sums[i]
                    own_sum = own_sum + for_query[part]
                    own_moment = own_moment + own_sum
                sums_ref[rows, :] = own_sum
                moments_ref[rows, :] = own_moment
            x, y = weights[half]
            for i in range(tiles):
                d = pl.ds(pl.multiple_of(at + i * 128, 128), 128)
                acc[0, :, d] += sums[i]
                acc[1, :, d] += sums[i] * x - moments[i]
                acc[2, :, d] += sums[i] * y
        return carry

    lax.fori_loop(0, BAND // 128 // tiles, chunk, 0, unroll=UNROLL if tops is None else 1)
    w = key_weights(sc)
    for piece in range(len(zs)):
        for slot in range(4):
            hi, lo = in_order((sums_ref, moments_ref), 4 * piece + slot)
            store(piece, slot, slice(0, 3), (nt_dot(w, hi) + nt_dot(w, lo))[0:3])


def spread_keys(sc, near, far, spread, acc, top=None):
    lane = iota((8, 128), 1) >> 4
    for stat in range(4):
        if stat == 3 and top is None:
            near[:, 3:4, :] = jnp.zeros((4, 1, 512), jnp.float32)
            far[:, 3:4, :] = jnp.zeros((4, 1, 512), jnp.float32)
            continue
        for part in range(4):
            out = jnp.zeros((8, 128), jnp.float32)
            for t in range(8):
                d = slice((part * 8 + t) * 128, (part * 8 + t) * 128 + 128)
                value = top[0:1, d] if stat == 3 else jnp.sum(acc[stat, :, d], 0, keepdims=True)
                value = pltpu.roll(jnp.broadcast_to(value, (8, 128)), 0, 1, stride=16, stride_axis=0)
                out = jnp.where(lane == t, pltpu.roll(value, (t * 16 + 16) % 128, 1), out)
            spread[:, part * 128 : part * 128 + 128] = out
        for i, ref in enumerate((near, far)):
            for j in range(4):
                row = 7 - ((sc[CORE] ^ i) * 4 + (sc[X] ^ j))
                ref[j, stat : stat + 1, :] = spread[pl.ds(row, 1), :]


def first_kernel(sc, ka, kb, q, kp, acc, rows, qp, sums_ref, moments_ref):
    set_keys(sc, ka, kb, kp)
    acc[...] = jnp.zeros_like(acc)
    set_queries([q], qp)

    def store(piece, slot, stats, value):
        rows[piece, slot, stats, :] = value

    block(sc, [sc[PIECE_Z]], qp, kp, acc, sums_ref, moments_ref, store)


def more_kernel(first, sc, kp, old, *refs):
    count = len(refs) - 5
    qs, (acc, rows, qp, sums_ref, moments_ref) = refs[:count], refs[count:]
    acc[...] = old[...]
    set_queries(qs, qp)

    def store(piece, slot, stats, value):
        rows[piece, slot, stats, :] = value

    zs = [sc[PIECE_Z + first + i] for i in range(count)]
    block(sc, zs, qp, kp, acc, sums_ref, moments_ref, store)


def last_kernel(sc, kp, old, q, r0, r1, r2, r3, *refs):
    pieces, refs = refs[:8], refs[8:]
    row_ref, near, far, acc, qp, sums_ref, moments_ref, spread, rm, km, raw, qx, sem = refs
    acc[...] = old[...]
    set_queries([q], qp)

    def place(piece, slot):
        return sc[PIECE_Z + piece] * 4 + (sc[Y] ^ slot)

    def store(piece, slot, stats, value):
        row_ref[place(piece, slot), stats, :] = value

    block(
        sc, [sc[PIECE_Z + 7]], qp, kp, acc, sums_ref, moments_ref,
        lambda _, *what: store(7, *what),
    )
    piece = 0
    for ref in (r0, r1, r2, r3):
        for i in range(ref.shape[0]):
            for slot in range(4):
                store(piece, slot, slice(0, 3), ref[i, slot, 0:3, :])
            piece += 1
    row_ref[:, 3:4, :] = jnp.zeros((32, 1, 128), jnp.float32)
    spread_keys(sc, near, far, spread, acc)
    sums = [row_ref[:, 0, :], near[:, 0, :], far[:, 0, :]]
    low = functools.reduce(jnp.minimum, [jnp.min(v) for v in sums])
    high = functools.reduce(jnp.maximum, [jnp.max(v) for v in sums])

    @pl.when(jnp.logical_not((low > LOW) & (high < HIGH)))
    def _():
        acc[...] = jnp.zeros_like(acc)
        km[...] = jnp.full_like(km, -jnp.inf)
        pick = jnp.where((iota((16, 128), 0) == 0) & (iota((16, 128), 1) == 0), 1.0, 0.0)
        pick = pick.astype(jnp.bfloat16)

        def fetch(piece):
            copy = pltpu.make_async_copy(pieces[piece], raw, sem)
            copy.start()
            copy.wait()
            set_queries([raw], qx, True)

        def block_top(half, t):
            lanes = pl.ds(pl.multiple_of(t * 128, 128), 128)
            s = nt_dot(qx[half * 256 : half * 256 + 256, :], kp[lanes, :]) * SCALE
            return lanes, s

        for piece in range(8):
            fetch(piece)

            def chunk(t, carry):
                for half in range(2):
                    lanes, s = block_top(half, t)
                    km[:, lanes] = jnp.maximum(km[:, lanes], jnp.max(s.reshape(RUN, 8, 128), 0))
                return carry

            lax.fori_loop(0, BAND // 128, chunk, 0)
        km[...] = jnp.broadcast_to(jnp.max(km[...], 0, keepdims=True), km.shape)
        for piece in range(8):
            fetch(piece)
            for half in range(2):

                def chunk(t, top, half=half):
                    return jnp.maximum(top, block_top(half, t)[1])

                top = jnp.full((256, 128), -jnp.inf, jnp.float32)
                top = lax.fori_loop(0, BAND // 128, chunk, top)
                hi, lo = split2(jnp.broadcast_to(jnp.max(top, 1, keepdims=True), (256, 128)))
                rm[half * 256 : half * 256 + 256, :] = hi.astype(jnp.float32) + lo.astype(
                    jnp.float32
                )
            for slot in range(4):
                hi, lo = in_order((rm,), slot)
                store(piece, slot, slice(3, 4), (nt_dot(pick, hi) + nt_dot(pick, lo))[0:1])
            block(
                sc, [sc[PIECE_Z + piece]], qx, kp, acc, sums_ref, moments_ref,
                lambda _, *what, piece=piece: store(piece, *what), (rm, km),
            )
        spread_keys(sc, near, far, spread, acc, km)


def merged(parts):
    top = parts[0][3:4]
    for part in parts[1:]:
        top = jnp.maximum(top, part[3:4])
    return sum(part[0:3] * jnp.exp2(part[3:4] - top) for part in parts), top


def merge_kernel(a, b, *outs):
    r, c = iota((512, 512), 0), iota((512, 512), 1)
    order = jnp.where(c == (r & 15) * RUN + (r >> 4), 1.0, 0.0).astype(jnp.bfloat16)
    rows = []
    for j in range(4):
        rows += list(merged([a[j], b[j]]))
    left = jnp.concatenate(rows, 0)
    parts = []
    for _ in range(3):
        parts.append(left.astype(jnp.bfloat16))
        left = left - parts[-1].astype(jnp.float32)
    got = jnp.dot(jnp.concatenate(parts, 0), order, preferred_element_type=jnp.float32)
    got = got[0:16] + got[16:32] + got[32:48]
    for j, out in enumerate(outs):
        out[...] = got[4 * j : 4 * j + 4]


def final_kernel(sc, rows, k0, k1, k2, k3, f_ref, b_ref):
    top = rows[:, 3, :]
    w = jnp.exp2(top - jnp.max(top, 0, keepdims=True))
    q = [jnp.sum(rows[:, stat, :] * w, 0, keepdims=True) for stat in range(3)]
    x, y = cell(query_base(sc[Z], sc[Y], sc[X], sc[CORE]) + iota((1, 128), 1))
    f_ref[0:1, :] = (q[1] / q[0] + (256.0 - x)) / FRAME_W
    f_ref[1:2, :] = (q[2] / q[0] + (128.0 - y)) / FRAME_W
    k, _ = merged([ref[...] for ref in (k0, k1, k2, k3)])
    x, y = cell(key_base(sc[Z], sc[Y], sc[X], sc[CORE]) + iota((1, 512), 1))
    b_ref[0:1, :] = (k[1:2] / k[0:1] + (256.0 - x)) / FRAME_W
    b_ref[1:2, :] = (k[2:3] / k[0:1] - y) / FRAME_W


def coords(i):
    out = {}
    for name in reversed(AXES):
        out[name] = i % SIZES[name]
        i //= SIZES[name]
    return out


def index(at):
    return functools.reduce(lambda a, name: a * SIZES[name] + at[name], AXES, 0)


def swap(value, **flips):
    def partner(i):
        at = coords(i)
        for name, flip in flips.items():
            at[name] ^= flip
        return index(at)

    return lax.ppermute(value, AXES, [(i, partner(i)) for i in range(256)])


def ring(value, odd):
    def partner(i):
        at = coords(i)
        z = (((at["zh"] * 2 + at["zl"] + odd) ^ 1) - odd) % 8
        at["zh"], at["zl"] = z // 2, z % 2
        return index(at)

    return lax.ppermute(value, AXES, [(i, partner(i)) for i in range(256)])


SMEM = pl.BlockSpec(memory_space=pltpu.SMEM)
VMEM = pl.BlockSpec(memory_space=pltpu.VMEM)
ANY = pl.BlockSpec(memory_space=pl.ANY)


def f32(*shape):
    return jax.ShapeDtypeStruct(shape, jnp.float32)


def call(kernel, name, args, in_specs, out_shape, scratch, pieces, alias=None):
    return pl.pallas_call(
        kernel,
        name=name,
        out_shape=out_shape,
        in_specs=in_specs,
        out_specs=[VMEM] * len(out_shape),
        scratch_shapes=scratch,
        input_output_aliases=alias or {},
        cost_estimate=pl.CostEstimate(
            flops=pieces * 2 * PIECE * BAND * 256, bytes_accessed=2**21, transcendentals=pieces * PIECE * BAND
        ),
        compiler_params=pltpu.CompilerParams(vmem_limit_bytes=40 * 2**20),
    )(*args)


def on_device(q, k):
    me = {name: lax.axis_index(name) for name in AXES}
    z = me["zh"] * 2 + me["zl"]
    by_y = [swap(q, y=j) for j in (1, 3, 2)]
    by_x = [swap(k, x=j) for j in (1, 3, 2)]
    by_y, by_x = lax.optimization_barrier((by_y, by_x))
    own = jnp.concatenate([q, by_y[0], by_y[2], by_y[1]])
    ka = jnp.concatenate([k, by_x[0], by_x[2], by_x[1]])
    kb = swap(ka, core=1)
    ahead = 1 - 2 * (z & 1)
    z_of = [(z + off * ahead) % 8 for off in (0, 1, -1, 2, -2, 3, -3, 4)]
    sc = jnp.stack([me["core"], me["x"], me["y"], z] + z_of).astype(jnp.int32)

    half_sums = [pltpu.VMEM((PIECE, 128), jnp.float32)] * 2
    piece_rows = pltpu.VMEM((PIECE, 2 * CH), jnp.bfloat16)
    plain = [pltpu.VMEM((PIECE, CH), jnp.bfloat16)] * 2
    two = [pltpu.VMEM((2 * PIECE, 2 * CH), jnp.bfloat16)] + [pltpu.VMEM((2 * PIECE, 128), jnp.float32)] * 2
    pieces = [own, ring(own, 0), ring(own, 1)]
    kp, acc, r0 = call(
        first_kernel, "first", (sc, ka, kb, own), [SMEM, VMEM, VMEM, VMEM],
        [jax.ShapeDtypeStruct((BAND, CH), jnp.bfloat16), f32(3, 8, BAND), f32(1, 4, 4, 128)],
        [piece_rows] + half_sums, 1,
    )
    parts = [r0]
    for first in (1, 3, 5):
        up, down, acc = lax.optimization_barrier((pieces[first], pieces[first + 1], acc))
        pieces += [ring(down, 0), ring(up, 1)] if first < 5 else [ring(down, 0)]
        acc, got = call(
            functools.partial(more_kernel, first), f"more{first}",
            (sc, kp, acc, up, down), [SMEM] + [VMEM] * 4,
            [f32(3, 8, BAND), f32(2, 4, 4, 128)], two, 2,
        )
        parts.append(got)
    rows, near, far = call(
        last_kernel, "last", (sc, kp, acc, pieces[7], *parts, *pieces),
        [SMEM] + [VMEM] * 7 + [ANY] * 8, [f32(32, 4, 128), f32(4, 4, 512), f32(4, 4, 512)],
        [pltpu.VMEM((3, 8, BAND), jnp.float32), piece_rows] + half_sums
        + [pltpu.VMEM((8, 512), jnp.float32), pltpu.VMEM((PIECE, 128), jnp.float32),
           pltpu.VMEM((8, BAND), jnp.float32), *plain, pltpu.SemaphoreType.DMA], 1,
    )
    cols = call(
        merge_kernel, "merge", (near, swap(far, core=1)), [VMEM] * 2, [f32(4, 512)] * 4, [], 0
    )
    cols = [cols[0]] + [swap(cols[j], x=j) for j in (1, 3, 2)]
    rows = lax.all_to_all(rows, ("zh", "zl", "y"), 0, 0)
    return call(
        final_kernel, "finish", (sc, rows, *cols), [SMEM] + [VMEM] * 5, [f32(2, 128), f32(2, 512)], [], 0
    )


def solution(mesh):
    fine = Mesh(mesh.devices.reshape(tuple(SIZES[name] for name in AXES)), AXES)
    key = ("zh", "x", "core", "zl", "y")
    return jax.shard_map(
        on_device,
        mesh=fine,
        in_specs=(P(AXES), P(key)),
        out_specs=(P(None, AXES), P(None, key)),
        check_vma=False,
    )
```

```python
import functools
import math

import jax
import jax.numpy as jnp
from jax import lax
from jax.experimental import pallas as pl
from jax.experimental.pallas import tpu as pltpu
from jax.sharding import Mesh
from jax.sharding import PartitionSpec as P

FRAME_W = 480
CH = 128
BAND = 4096
PIECE = 512
RUN = 32
TILES = 4
UNROLL = 8
SCALE = math.log2(math.e) / math.sqrt(CH)
LOW, HIGH = 2.0**-90, 2.0**100
AXES = ("zl", "y", "zh", "x", "core")
SIZES = {"zl": 2, "y": 4, "zh": 4, "x": 4, "core": 2}
NT = (((1,), (1,)), ((), ()))
CORE, X, Y, Z, PIECE_Z = 0, 1, 2, 3, 4


def nt_dot(a, b):
    return lax.dot_general(a, b, NT, preferred_element_type=jnp.float32)


def split2(v):
    high = v.astype(jnp.bfloat16)
    return high, (v - high.astype(jnp.float32)).astype(jnp.bfloat16)


def cell(n):
    y = ((n >> 5) * 4370) >> 16
    return (n - y * FRAME_W).astype(jnp.float32), y.astype(jnp.float32)


def iota(shape, axis):
    return lax.broadcasted_iota(jnp.int32, shape, axis)


def key_base(z, y, x, core):
    return ((((z >> 1) * 4 + x) * 2 + core) * 8 + (z & 1) * 4 + y) * 512


def query_base(z, y, x, core):
    return ((((z & 1) * 4 + y) * 4 + (z >> 1)) * 8 + x * 2 + core) * 128


def key_weights(sc):
    lane = iota((16, 256), 1)
    row = iota((16, 256), 0)
    on_sum = lane < 128
    s, g = (lane >> 4) & 7, lane & 15
    x, y = cell(key_base(sc[Z], sc[Y], s & 3, s >> 2) + g * RUN)
    x, y = x + (RUN - 256.0), y - 128.0
    value = jnp.where(row == 0, 1.0, jnp.where(row == 1, x, jnp.where(row == 2, y, 0.0)))
    value = jnp.where(on_sum, value, jnp.where(row == 1, -1.0, 0.0))
    return value.astype(jnp.bfloat16)


def query_weights(sc, z, half):
    r = iota((8, 128), 0)
    slot = jnp.where(r < 4, 2 * half, 2 * half + 1)
    x, y = cell(query_base(z, sc[Y] ^ slot, sc[X], sc[CORE]) + (r & 3) * RUN)
    return x + (RUN - 256.0), y


def run_order():
    r, c = iota((256, 256), 0), iota((256, 256), 1)
    return jnp.where(c == (r & 7) * RUN + (r >> 3), 1.0, 0.0).astype(jnp.bfloat16)


def set_keys(sc, ka, kb, kp):
    perm = run_order()
    for core, ref in ((sc[CORE], ka), (1 - sc[CORE], kb)):
        for j in range(4):
            shard = core * 4 + (sc[X] ^ j)
            low, high = (
                jnp.dot(perm, ref[at : at + 256, :], preferred_element_type=jnp.float32)
                for at in (j * 512, j * 512 + 256)
            )
            for t in range(RUN):
                rows = jnp.concatenate([low[t * 8 : t * 8 + 8], high[t * 8 : t * 8 + 8]], 0)
                at = pl.multiple_of(t * 128 + shard * 16, 16)
                kp[pl.ds(at, 16), :] = rows.astype(jnp.bfloat16)


def set_queries(refs, qp, plain=False):
    perm = run_order()
    for i, ref in enumerate(refs):
        for half in range(2):
            rows = slice(half * 256, half * 256 + 256)
            got = jnp.dot(perm, ref[rows, :], preferred_element_type=jnp.float32)
            to = slice(i * PIECE + half * 256, i * PIECE + half * 256 + 256)
            if plain:
                qp[to, :] = got.astype(jnp.bfloat16)
            else:
                qp[to, 0:CH], qp[to, CH : 2 * CH] = split2(got * SCALE)


def in_order(refs, part):
    got = []
    for run in range(4 * part, 4 * part + 4):
        there = pl.ds((run // 8) * 256 + run % 8, RUN, stride=8)
        got.append(jnp.concatenate([ref[there, :] for ref in refs], 1))
    return split2(jnp.concatenate(got, 0))


def block(sc, zs, qp, kp, acc, sums_ref, moments_ref, store, tops=None):
    tiles = TILES if tops is None else 1
    halves = 2 * len(zs)
    sums_ref[...] = jnp.zeros_like(sums_ref)
    moments_ref[...] = jnp.zeros_like(moments_ref)
    weights = [query_weights(sc, zs[half // 2], half % 2) for half in range(halves)]

    def chunk(j, carry):
        at = pl.multiple_of(j * tiles * 128, tiles * 128)
        lanes = pl.ds(at, tiles * 128)
        if tops is None:
            keys = kp[lanes, :]
            s = nt_dot(qp[0 : halves * 256, :], jnp.concatenate([keys, keys], 1))
            for_query = for_key = jnp.exp2(s)
        else:
            s = nt_dot(qp[...], kp[lanes, :]) * SCALE
            for_query = jnp.exp2(s - tops[0][...])
            for_key = jnp.exp2(s - tops[1][0:1, lanes])
        for half in range(halves):
            sums, moments = [None] * tiles, [None] * tiles
            for u in range(RUN):
                rows = slice(half * 256 + u * 8, half * 256 + u * 8 + 8)
                own_sum, own_moment = sums_ref[rows, :], moments_ref[rows, :]
                for i in range(tiles):
                    part = (rows, slice(i * 128, i * 128 + 128))
                    e = for_key[part]
                    sums[i] = e if u == 0 else sums[i] + e
                    moments[i] = sums[i] if u == 0 else moments[i] + sums[i]
                    own_sum = own_sum + for_query[part]
                    own_moment = own_moment + own_sum
                sums_ref[rows, :] = own_sum
                moments_ref[rows, :] = own_moment
            x, y = weights[half]
            for i in range(tiles):
                d = pl.ds(pl.multiple_of(at + i * 128, 128), 128)
                acc[0, :, d] += sums[i]
                acc[1, :, d] += sums[i] * x - moments[i]
                acc[2, :, d] += sums[i] * y
        return carry

    lax.fori_loop(0, BAND // 128 // tiles, chunk, 0, unroll=UNROLL if tops is None else 1)
    w = key_weights(sc)
    for piece in range(len(zs)):
        for slot in range(4):
            hi, lo = in_order((sums_ref, moments_ref), 4 * piece + slot)
            store(piece, slot, slice(0, 3), (nt_dot(w, hi) + nt_dot(w, lo))[0:3])


def spread_keys(sc, near, far, spread, acc, top=None):
    lane = iota((8, 128), 1) >> 4
    for stat in range(4):
        if stat == 3 and top is None:
            near[:, 3:4, :] = jnp.zeros((4, 1, 512), jnp.float32)
            far[:, 3:4, :] = jnp.zeros((4, 1, 512), jnp.float32)
            continue
        for part in range(4):
            out = jnp.zeros((8, 128), jnp.float32)
            for t in range(8):
                d = slice((part * 8 + t) * 128, (part * 8 + t) * 128 + 128)
                value = top[0:1, d] if stat == 3 else jnp.sum(acc[stat, :, d], 0, keepdims=True)
                value = pltpu.roll(jnp.broadcast_to(value, (8, 128)), 0, 1, stride=16, stride_axis=0)
                out = jnp.where(lane == t, pltpu.roll(value, (t * 16 + 16) % 128, 1), out)
            spread[:, part * 128 : part * 128 + 128] = out
        for i, ref in enumerate((near, far)):
            for j in range(4):
                row = 7 - ((sc[CORE] ^ i) * 4 + (sc[X] ^ j))
                ref[j, stat : stat + 1, :] = spread[pl.ds(row, 1), :]


def first_kernel(sc, ka, kb, q, kp, acc, rows, qp, sums_ref, moments_ref):
    set_keys(sc, ka, kb, kp)
    acc[...] = jnp.zeros_like(acc)
    set_queries([q], qp)

    def store(piece, slot, stats, value):
        rows[piece, slot, stats, :] = value

    block(sc, [sc[PIECE_Z]], qp, kp, acc, sums_ref, moments_ref, store)


def more_kernel(first, sc, kp, old, *refs):
    count = len(refs) - 5
    qs, (acc, rows, qp, sums_ref, moments_ref) = refs[:count], refs[count:]
    acc[...] = old[...]
    set_queries(qs, qp)

    def store(piece, slot, stats, value):
        rows[piece, slot, stats, :] = value

    zs = [sc[PIECE_Z + first + i] for i in range(count)]
    block(sc, zs, qp, kp, acc, sums_ref, moments_ref, store)


def last_kernel(sc, kp, old, q, r0, r1, r2, r3, *refs):
    pieces, refs = refs[:8], refs[8:]
    row_ref, near, far, acc, qp, sums_ref, moments_ref, spread, rm, km, raw, qx, sem = refs
    acc[...] = old[...]
    set_queries([q], qp)

    def place(piece, slot):
        return sc[PIECE_Z + piece] * 4 + (sc[Y] ^ slot)

    def store(piece, slot, stats, value):
        row_ref[place(piece, slot), stats, :] = value

    block(
        sc, [sc[PIECE_Z + 7]], qp, kp, acc, sums_ref, moments_ref,
        lambda _, *what: store(7, *what),
    )
    piece = 0
    for ref in (r0, r1, r2, r3):
        for i in range(ref.shape[0]):
            for slot in range(4):
                store(piece, slot, slice(0, 3), ref[i, slot, 0:3, :])
            piece += 1
    row_ref[:, 3:4, :] = jnp.zeros((32, 1, 128), jnp.float32)
    spread_keys(sc, near, far, spread, acc)
    sums = [row_ref[:, 0, :], near[:, 0, :], far[:, 0, :]]
    low = functools.reduce(jnp.minimum, [jnp.min(v) for v in sums])
    high = functools.reduce(jnp.maximum, [jnp.max(v) for v in sums])

    @pl.when(jnp.logical_not((low > LOW) & (high < HIGH)))
    def _():
        acc[...] = jnp.zeros_like(acc)
        km[...] = jnp.full_like(km, -jnp.inf)
        pick = jnp.where((iota((16, 128), 0) == 0) & (iota((16, 128), 1) == 0), 1.0, 0.0)
        pick = pick.astype(jnp.bfloat16)

        def fetch(piece):
            copy = pltpu.make_async_copy(pieces[piece], raw, sem)
            copy.start()
            copy.wait()
            set_queries([raw], qx, True)

        def block_top(half, t):
            lanes = pl.ds(pl.multiple_of(t * 128, 128), 128)
            s = nt_dot(qx[half * 256 : half * 256 + 256, :], kp[lanes, :]) * SCALE
            return lanes, s

        for piece in range(8):
            fetch(piece)

            def chunk(t, carry):
                for half in range(2):
                    lanes, s = block_top(half, t)
                    km[:, lanes] = jnp.maximum(km[:, lanes], jnp.max(s.reshape(RUN, 8, 128), 0))
                return carry

            lax.fori_loop(0, BAND // 128, chunk, 0)
        km[...] = jnp.broadcast_to(jnp.max(km[...], 0, keepdims=True), km.shape)
        for piece in range(8):
            fetch(piece)
            for half in range(2):

                def chunk(t, top, half=half):
                    return jnp.maximum(top, block_top(half, t)[1])

                top = jnp.full((256, 128), -jnp.inf, jnp.float32)
                top = lax.fori_loop(0, BAND // 128, chunk, top)
                hi, lo = split2(jnp.broadcast_to(jnp.max(top, 1, keepdims=True), (256, 128)))
                rm[half * 256 : half * 256 + 256, :] = hi.astype(jnp.float32) + lo.astype(
                    jnp.float32
                )
            for slot in range(4):
                hi, lo = in_order((rm,), slot)
                store(piece, slot, slice(3, 4), (nt_dot(pick, hi) + nt_dot(pick, lo))[0:1])
            block(
                sc, [sc[PIECE_Z + piece]], qx, kp, acc, sums_ref, moments_ref,
                lambda _, *what, piece=piece: store(piece, *what), (rm, km),
            )
        spread_keys(sc, near, far, spread, acc, km)


def merged(parts):
    top = parts[0][3:4]
    for part in parts[1:]:
        top = jnp.maximum(top, part[3:4])
    return sum(part[0:3] * jnp.exp2(part[3:4] - top) for part in parts), top


def merge_kernel(a, b, *outs):
    r, c = iota((512, 512), 0), iota((512, 512), 1)
    order = jnp.where(c == (r & 15) * RUN + (r >> 4), 1.0, 0.0).astype(jnp.bfloat16)
    rows = []
    for j in range(4):
        rows += list(merged([a[j], b[j]]))
    left = jnp.concatenate(rows, 0)
    parts = []
    for _ in range(3):
        parts.append(left.astype(jnp.bfloat16))
        left = left - parts[-1].astype(jnp.float32)
    got = jnp.dot(jnp.concatenate(parts, 0), order, preferred_element_type=jnp.float32)
    got = got[0:16] + got[16:32] + got[32:48]
    for j, out in enumerate(outs):
        out[...] = got[4 * j : 4 * j + 4]


def final_kernel(sc, rows, k0, k1, k2, k3, f_ref, b_ref):
    top = rows[:, 3, :]
    w = jnp.exp2(top - jnp.max(top, 0, keepdims=True))
    q = [jnp.sum(rows[:, stat, :] * w, 0, keepdims=True) for stat in range(3)]
    x, y = cell(query_base(sc[Z], sc[Y], sc[X], sc[CORE]) + iota((1, 128), 1))
    f_ref[0:1, :] = (q[1] / q[0] + (256.0 - x)) / FRAME_W
    f_ref[1:2, :] = (q[2] / q[0] + (128.0 - y)) / FRAME_W
    k, _ = merged([ref[...] for ref in (k0, k1, k2, k3)])
    x, y = cell(key_base(sc[Z], sc[Y], sc[X], sc[CORE]) + iota((1, 512), 1))
    b_ref[0:1, :] = (k[1:2] / k[0:1] + (256.0 - x)) / FRAME_W
    b_ref[1:2, :] = (k[2:3] / k[0:1] - y) / FRAME_W


def coords(i):
    out = {}
    for name in reversed(AXES):
        out[name] = i % SIZES[name]
        i //= SIZES[name]
    return out


def index(at):
    return functools.reduce(lambda a, name: a * SIZES[name] + at[name], AXES, 0)


def swap(value, **flips):
    def partner(i):
        at = coords(i)
        for name, flip in flips.items():
            at[name] ^= flip
        return index(at)

    return lax.ppermute(value, AXES, [(i, partner(i)) for i in range(256)])


def ring(value, odd):
    def partner(i):
        at = coords(i)
        z = (((at["zh"] * 2 + at["zl"] + odd) ^ 1) - odd) % 8
        at["zh"], at["zl"] = z // 2, z % 2
        return index(at)

    return lax.ppermute(value, AXES, [(i, partner(i)) for i in range(256)])


SMEM = pl.BlockSpec(memory_space=pltpu.SMEM)
VMEM = pl.BlockSpec(memory_space=pltpu.VMEM)
ANY = pl.BlockSpec(memory_space=pl.ANY)


def f32(*shape):
    return jax.ShapeDtypeStruct(shape, jnp.float32)


def call(kernel, name, args, in_specs, out_shape, scratch, pieces, alias=None):
    return pl.pallas_call(
        kernel,
        name=name,
        out_shape=out_shape,
        in_specs=in_specs,
        out_specs=[VMEM] * len(out_shape),
        scratch_shapes=scratch,
        input_output_aliases=alias or {},
        cost_estimate=pl.CostEstimate(
            flops=pieces * 2 * PIECE * BAND * 256, bytes_accessed=2**21, transcendentals=pieces * PIECE * BAND
        ),
        compiler_params=pltpu.CompilerParams(vmem_limit_bytes=40 * 2**20),
    )(*args)


def on_device(q, k):
    me = {name: lax.axis_index(name) for name in AXES}
    z = me["zh"] * 2 + me["zl"]
    by_y = [swap(q, y=j) for j in (1, 3, 2)]
    by_x = [swap(k, x=j) for j in (1, 3, 2)]
    by_y, by_x = lax.optimization_barrier((by_y, by_x))
    own = jnp.concatenate([q, by_y[0], by_y[2], by_y[1]])
    ka = jnp.concatenate([k, by_x[0], by_x[2], by_x[1]])
    kb = swap(ka, core=1)
    ahead = 1 - 2 * (z & 1)
    z_of = [(z + off * ahead) % 8 for off in (0, -1, 1, -2, 2, -3, 3, 4)]
    sc = jnp.stack([me["core"], me["x"], me["y"], z] + z_of).astype(jnp.int32)

    half_sums = [pltpu.VMEM((PIECE, 128), jnp.float32)] * 2
    piece_rows = pltpu.VMEM((PIECE, 2 * CH), jnp.bfloat16)
    plain = [pltpu.VMEM((PIECE, CH), jnp.bfloat16)] * 2
    two = [pltpu.VMEM((2 * PIECE, 2 * CH), jnp.bfloat16)] + [pltpu.VMEM((2 * PIECE, 128), jnp.float32)] * 2
    pieces = [own, ring(own, 1), ring(own, 0)]
    kp, acc, r0 = call(
        first_kernel, "first", (sc, ka, kb, own), [SMEM, VMEM, VMEM, VMEM],
        [jax.ShapeDtypeStruct((BAND, CH), jnp.bfloat16), f32(3, 8, BAND), f32(1, 4, 4, 128)],
        [piece_rows] + half_sums, 1,
    )
    parts = [r0]
    for first in (1, 3, 5):
        up, down, acc = lax.optimization_barrier((pieces[first], pieces[first + 1], acc))
        pieces += [ring(down, 1), ring(up, 0)] if first < 5 else [ring(up, 0)]
        acc, got = call(
            functools.partial(more_kernel, first), f"more{first}",
            (sc, kp, acc, up, down), [SMEM] + [VMEM] * 4,
            [f32(3, 8, BAND), f32(2, 4, 4, 128)], two, 2,
        )
        parts.append(got)
    rows, near, far = call(
        last_kernel, "last", (sc, kp, acc, pieces[7], *parts, *pieces),
        [SMEM] + [VMEM] * 7 + [ANY] * 8, [f32(32, 4, 128), f32(4, 4, 512), f32(4, 4, 512)],
        [pltpu.VMEM((3, 8, BAND), jnp.float32), piece_rows] + half_sums
        + [pltpu.VMEM((8, 512), jnp.float32), pltpu.VMEM((PIECE, 128), jnp.float32),
           pltpu.VMEM((8, BAND), jnp.float32), *plain, pltpu.SemaphoreType.DMA], 1,
    )
    cols = call(
        merge_kernel, "merge", (near, swap(far, core=1)), [VMEM] * 2, [f32(4, 512)] * 4, [], 0
    )
    cols = [cols[0]] + [swap(cols[j], x=j) for j in (1, 3, 2)]
    rows = lax.all_to_all(rows, ("zh", "zl", "y"), 0, 0)
    return call(
        final_kernel, "finish", (sc, rows, *cols), [SMEM] + [VMEM] * 5, [f32(2, 128), f32(2, 512)], [], 0
    )


def solution(mesh):
    fine = Mesh(mesh.devices.reshape(tuple(SIZES[name] for name in AXES)), AXES)
    key = ("zh", "x", "core", "zl", "y")
    return jax.shard_map(
        on_device,
        mesh=fine,
        in_specs=(P(AXES), P(key)),
        out_specs=(P(None, AXES), P(None, key)),
        check_vma=False,
    )
```
